1024 devices in a mesh: dp: 128 (over z, y_lo, x), tensor: 8 (over y_hi, core).
Axes of the slice: x: 4, y: 8 (y_hi: 4, y_lo: 2; y = y_hi * 2 + y_lo), z: 16, core: 2. Of those that a mesh axis runs over, the one named last changes fastest.
Arguments:
- rollout_states: bfloat16 [32768, 4096], P('dp', 'tensor'), may hold values from -6 to 6
- lengths: int32 [128, 4], P('dp'), may hold values from 1 to 192, 256 in all within a row
- moved: int32 [128], P('dp'), may hold values from 0 to 3, as said below
- norm_gain: bfloat16 [4096], replicated, may hold values from 0.099609375 to 1.8984375
- qkv_weight: bfloat16 [4096, 6144], P('dp', 'tensor'), may hold values from -0.09375 to 0.09375
- qkv_bias: bfloat16 [6144], P('tensor'), may hold values from -5 to 5
Outputs:
- context: bfloat16 [65536, 4096], P('dp', 'tensor')
The draws below stay inside these ranges and needn't reach their ends.
Inputs may be any that keep to these rules, and one draw needn't show every extreme that they name: `moved`: the last rollout group keeps all of its responses; every other group hands on at least one.
All inputs are finite; a program needn't handle non-finite values.
Results may differ from the reference program's by a relative error of at most 0.011.
Values may be sent and summed in bfloat16 or wider, within the bound.
No kernel may reach another device: no remote copies, remote signals or barrier semaphores. Data moves between devices by JAX's collectives and lax.ppermute only.
A program may use at most 32 MiB of HBM per device.

```python
import math
import jax
import jax.numpy as jnp
import numpy as np
from jax import lax

D = 4096
HEADS = 32
KV = 8
HEAD = 128
RTOK = 256
SAMP_DEV = 4
GROUPS = 128
QKV_COLS = 6144
MAXLEN = 192
TOKENS = 32768


def draw_moved(key, part):
    key = jax.random.fold_in(key, 7)
    counts = jax.random.randint(key, (GROUPS,), 1, SAMP_DEV)
    counts = counts.at[0].set(SAMP_DEV - 1)
    counts = counts.at[GROUPS - 1].set(0)
    return counts.astype(jnp.int32)


def draw_qkv_bias(key, part):
    key = jax.random.fold_in(key, 11)
    jitter_key = jax.random.fold_in(key, 0)
    per_group = HEADS // KV
    layout = (KV, per_group + 2, HEAD)
    offsets = jnp.clip(0.5 * jax.random.normal(jitter_key, layout, jnp.float32), -2.5, 2.5)
    return offsets.reshape(-1).astype(jnp.bfloat16)


def block_levels(rng, shape, cuts, low, high):
    loudness, own = 1.0, jax.random.fold_in(rng, 6)
    for axis_at, shards_of in cuts:
        heights = jnp.exp(jax.random.uniform(jax.random.fold_in(own, axis_at), (shards_of,), jnp.float32, low / len(cuts), high / len(cuts)))
        loudness = loudness * jnp.repeat(heights, shape[axis_at] // shards_of).reshape([-1 if axis == axis_at else 1 for axis in range(len(shape))])
    return loudness


def profile(amount, total, most, lean):
    portions = [(1 << 20) // math.isqrt(standing ** lean) + 1 for standing in range(2, amount + 1)]
    spare, holding = total - most - (amount - 1), [1] * (amount - 1)
    while spare > 0:
        candidates = [i for i in range(amount - 1) if holding[i] < most]
        mass, left = sum([portions[i] for i in candidates]), spare
        for i in candidates:
            more = min(most - holding[i], max(1, left * portions[i] // mass), spare)
            holding[i] = holding[i] + more
            spare = spare - more
    return np.array([most] + holding)


def uneven_parts(rng, count, total, bound, slope):
    if count == 2:
        one = jax.random.randint(rng, (), max(1, total - bound), min(bound, total - 1) + 1)
        return jnp.stack([one, total - one])
    tallies = jnp.asarray(profile(count, total, bound, slope), jnp.int32)
    twos = (count - 1) // 2
    donor, taker = tallies[1:1 + 2 * twos:2], tallies[2:2 + 2 * twos:2]
    slack = jnp.minimum(donor - 1, bound - taker)
    moved = jax.random.randint(jax.random.fold_in(rng, 1), (twos,), 0, 1 << 20) % (slack + 1)
    tallies = tallies.at[1:1 + 2 * twos:2].set(donor - moved).at[2:2 + 2 * twos:2].set(taker + moved)
    return tallies[jax.random.permutation(jax.random.fold_in(rng, 2), count)]


def scatter_about(stream_key, shape, scale, limit, pieces=(), kind=jnp.bfloat16):
    drawn = jax.random.normal(stream_key, shape, jnp.float32) * scale
    if len(pieces) > 0:
        drawn = block_levels(stream_key, shape, pieces, -0.22, 0.18) * drawn
    return jnp.clip(drawn, min=-limit, max=limit).astype(kind)


def setup_inputs(seed: int = 0) -> dict:
    keys = jax.random.split(jax.random.key(seed), 7)
    return {
        "rollout_states": scatter_about(keys[0], (TOKENS, D), 1.0, 6.0, ((0, 128), (1, 8))),
        "lengths": jax.vmap(lambda own: uneven_parts(own, SAMP_DEV, RTOK, MAXLEN, 2))(jax.random.split(keys[1], GROUPS)).reshape((GROUPS, SAMP_DEV)).astype(jnp.int32),
        "moved": draw_moved(jax.random.fold_in(keys[6], 71), 0),
        "norm_gain": jnp.clip(1.0 + 0.18 * jax.random.normal(keys[3], (D,), jnp.float32), 0.099609375, 1.8984375).astype(jnp.bfloat16),
        "qkv_weight": scatter_about(keys[4], (D, QKV_COLS), D ** -0.5, 0.09375, ((0, 128), (1, 8))),
        "qkv_bias": draw_qkv_bias(jax.random.fold_in(keys[6], 71), 0),
    }


EPSILON = 1e-06
ROPE_BASE = 1000000.0

def token_layout(lengths_row, moved_count, slot_count):
    slot_ids = jnp.arange(slot_count, dtype=jnp.int32)
    samples = lengths_row.shape[0]
    starts = (jnp.cumsum(lengths_row) - lengths_row).astype(jnp.int32)
    owners = lax.optimization_barrier(jnp.sum((starts[None, :] <= slot_ids[:, None]).astype(jnp.int32), axis=1)) - 1
    onehot = owners[:, None] == jnp.arange(samples, dtype=jnp.int32)[None, :]
    positions = slot_ids - lax.optimization_barrier(jnp.sum(jnp.where(onehot, starts[None, :], 0), axis=1))
    moving = jnp.arange(samples, dtype=jnp.int32) >= samples - moved_count
    tail_tokens = jnp.sum(jnp.where(moving, lengths_row, 0)).astype(jnp.int32)
    return (owners.astype(jnp.int32), positions.astype(jnp.int32), tail_tokens)

def project(states, norm_gain, qkv_weight, qkv_bias):
    values = states.astype(jnp.float32)
    mean_square = lax.optimization_barrier(jnp.mean(values * values, axis=1, keepdims=True))
    normed = (values * lax.rsqrt(mean_square + EPSILON) * norm_gain.astype(jnp.float32)).astype(jnp.bfloat16)
    projected = jnp.dot(normed, qkv_weight, preferred_element_type=jnp.float32)
    return projected + qkv_bias.astype(jnp.float32)

def rope_tables(positions):
    half_dim = HEAD // 2
    inv_freq = ROPE_BASE ** (-(2.0 * jnp.arange(half_dim, dtype=jnp.float32)) / HEAD)
    angles = positions.astype(jnp.float32)[:, None] * inv_freq[None, :]
    angles = jnp.concatenate([angles, angles], axis=1)
    return (jnp.cos(angles), jnp.sin(angles))

def rotary(values, cosine_table, sine_table):
    half_dim = values.shape[-1] // 2
    turned = jnp.concatenate([-values[..., half_dim:], values[..., :half_dim]], axis=-1)
    return values * cosine_table + turned * sine_table

def attend(projected, segments, positions):
    row_count = projected.shape[0]
    per_group = HEADS // KV
    groups = projected.shape[1] // ((per_group + 2) * HEAD)
    heads_view = projected.reshape(row_count, groups, per_group + 2, HEAD)
    cosine_table, sine_table = rope_tables(positions)
    query_heads = rotary(heads_view[:, :, :per_group], cosine_table[:, None, None, :], sine_table[:, None, None, :]).astype(jnp.bfloat16)
    key_heads = rotary(heads_view[:, :, per_group], cosine_table[:, None, :], sine_table[:, None, :]).astype(jnp.bfloat16)
    value_heads = heads_view[:, :, per_group + 1].astype(jnp.bfloat16)
    scores = jnp.einsum('qgnd,kgd->gnqk', query_heads.astype(jnp.float32), key_heads.astype(jnp.float32)) * HEAD ** (-0.5)
    slot_ids = jnp.arange(row_count, dtype=jnp.int32)
    allowed = (segments[:, None] == segments[None, :]) & (slot_ids[None, :] <= slot_ids[:, None])
    scores = jnp.where(allowed[None, None], scores, -1e+30)
    row_max = lax.optimization_barrier(jnp.max(scores, axis=-1, keepdims=True))
    exp_scores = jnp.exp(scores - row_max)
    weights = (exp_scores / lax.optimization_barrier(jnp.sum(exp_scores, axis=-1, keepdims=True))).astype(jnp.bfloat16)
    context = jnp.einsum('gnqk,kgd->qgnd', weights.astype(jnp.float32), value_heads.astype(jnp.float32))
    return context.reshape(row_count, groups * per_group * HEAD).astype(jnp.bfloat16)

def assemble(previous, current, incoming, outgoing, pad_value):
    slot_count = current.shape[0]
    filler = jnp.full(current.shape, pad_value, current.dtype)
    stacked = jnp.concatenate([previous, current, filler], axis=0)
    packed = lax.dynamic_slice_in_dim(stacked, (slot_count - incoming).astype(jnp.int32), 2 * slot_count, 0)
    keep_mask = jnp.arange(2 * slot_count, dtype=jnp.int32) < incoming + slot_count - outgoing
    keep_mask = keep_mask.reshape((2 * slot_count,) + (1,) * (current.ndim - 1))
    return jnp.where(keep_mask, packed, jnp.asarray(pad_value, current.dtype))

def reference(rollout_states, lengths, moved, norm_gain, qkv_weight, qkv_bias):
    groups = lengths.shape[0]
    grouped = rollout_states.reshape(groups, RTOK, D)

    def one_group(items):
        owners, positions, tail_tokens = token_layout(items[1], items[2], RTOK)
        projected = project(items[0], norm_gain, qkv_weight, qkv_bias)
        return (attend(projected, owners, positions), tail_tokens)
    contexts, tails = lax.map(one_group, (grouped, lengths, moved))
    previous = jnp.concatenate([jnp.zeros_like(contexts[:1]), contexts[:-1]], axis=0)
    incoming = jnp.concatenate([jnp.zeros((1,), jnp.int32), tails[:-1]], axis=0)

    def one_row(items):
        return assemble(items[0], items[1], items[2], items[3], 0.0)
    packed = lax.map(one_row, (previous, contexts, incoming, tails))
    return packed.reshape(groups * 2 * RTOK, HEADS * HEAD)
```

```python
import functools

import jax
import jax.numpy as jnp
from jax import lax
from jax.experimental import pallas as pl
from jax.experimental.pallas import tpu as pltpu
from jax.sharding import Mesh
from jax.sharding import PartitionSpec as P

HEADS = 32
KV = 8
HEAD = 128
PER = HEADS // KV
EPSILON = 1e-06
ROPE_BASE = 1000000.0

NZ, NYL, NX, NYH, NC = 16, 2, 4, 4, 2
DP = ("z", "yl", "x")
TP = ("yh", "c")
WROWS = 32
ROWS = 256
VMEM = 32 << 20


def whole(shape):
    return pl.BlockSpec(memory_space=pltpu.VMEM)


def call(kernel, out_shape, args, scalars=0, flops=0, nbytes=0, scratch=()):
    smem = pl.BlockSpec(memory_space=pltpu.SMEM)
    vmem = pl.BlockSpec(memory_space=pltpu.VMEM)
    return pl.pallas_call(
        kernel,
        out_shape=out_shape,
        in_specs=[smem] * scalars + [vmem] * (len(args) - scalars),
        out_specs=vmem if not isinstance(out_shape, (list, tuple)) else [vmem] * len(out_shape),
        scratch_shapes=list(scratch),
        compiler_params=pltpu.CompilerParams(vmem_limit_bytes=VMEM),
        cost_estimate=pl.CostEstimate(flops=flops, bytes_accessed=nbytes, transcendentals=0),
    )(*args)


def reorder_kernel(yl_ref, s_ref, o_ref):
    yl = yl_ref[0]
    source = lax.broadcasted_iota(jnp.int32, (512, 128), 0)
    r = lax.broadcasted_iota(jnp.int32, (512, 128), 1)
    rel, zz, k = lax.shift_right_logical(r, 6), lax.shift_right_logical(r, 5) & 1, r & 31
    base = zz * 256 + (rel ^ yl) * 128 + k
    for x in range(NX):
        perm = (source == base + x * 32).astype(jnp.bfloat16)
        o_ref[x] = jnp.dot(s_ref[...], perm, preferred_element_type=jnp.float32).astype(jnp.bfloat16)


def matmul_kernel(c_ref, own_ref, oth_ref, wown_ref, woth_ref, o_ref, w_ref):
    c = c_ref[0]
    for rel in range(NC):
        for yh in range(NYH):
            row = pl.multiple_of((yh * 4 + (c ^ rel) * 2) * WROWS, 64)
            at = (rel * NYH + yh) * 128
            w_ref[at : at + 64] = wown_ref[pl.ds(row, 64)]
            w_ref[at + 64 : at + 128] = woth_ref[pl.ds(row, 64)]

    def body(g, carry):
        rows = pl.ds(pl.multiple_of(g * ROWS, ROWS), ROWS)
        x = jnp.concatenate(
            [own_ref[yh, rows] for yh in range(NYH)] + [oth_ref[yh, rows] for yh in range(NYH)], axis=1
        )
        o_ref[g] = jnp.dot(x, w_ref[...], preferred_element_type=jnp.float32).astype(jnp.bfloat16)
        return carry

    lax.fori_loop(0, NX, body, 0)


def attend_kernel(len_ref, a_ref, b_ref, r_ref, bias_ref, cos_ref, sin_ref, o_ref):
    s1 = len_ref[0]
    s2 = s1 + len_ref[1]
    s3 = s2 + len_ref[2]
    i = lax.broadcasted_iota(jnp.int32, (ROWS, ROWS), 0)
    j = lax.broadcasted_iota(jnp.int32, (ROWS, ROWS), 1)
    start = jnp.where(i >= s3, s3, jnp.where(i >= s2, s2, jnp.where(i >= s1, s1, 0)))
    allowed = (j >= start) & (j <= i)
    r = r_ref[...]
    cos, sin = cos_ref[...], sin_ref[...]

    def head(n):
        ref, at = (a_ref, n * HEAD) if n < 3 else (b_ref, (n - 3) * HEAD)
        total = ref[0, :, at : at + HEAD].astype(jnp.float32)
        for k in range(1, NX):
            total = total + ref[k, :, at : at + HEAD].astype(jnp.float32)
        return total * r + bias_ref[:, n * HEAD : (n + 1) * HEAD]

    def rotate(v):
        return (v * cos + pltpu.roll(v, HEAD // 2, 1) * sin).astype(jnp.bfloat16)

    key = rotate(head(PER))
    value = head(PER + 1).astype(jnp.bfloat16)
    for h in range(PER):
        query = rotate(head(h))
        scores = lax.dot_general(query, key, (((1,), (1,)), ((), ())), preferred_element_type=jnp.float32)
        scores = jnp.where(allowed, scores * HEAD ** (-0.5), -1e30)
        e = jnp.exp(scores - jnp.max(scores, axis=1, keepdims=True))
        weights = (e / jnp.sum(e, axis=1, keepdims=True)).astype(jnp.bfloat16)
        o_ref[:, h * HEAD : (h + 1) * HEAD] = jnp.dot(
            weights, value, preferred_element_type=jnp.float32
        ).astype(jnp.bfloat16)


def pack_kernel(n_ref, prev_ref, own_ref, o_ref):
    incoming, tail = n_ref[0], n_ref[1]
    slot = lax.broadcasted_iota(jnp.int32, (2 * ROWS, ROWS), 0)
    row = lax.broadcasted_iota(jnp.int32, (2 * ROWS, ROWS), 1)
    first = ((slot < incoming) & (row == slot + (ROWS - incoming))).astype(jnp.bfloat16)
    second = ((row == slot - incoming) & (row < ROWS - tail)).astype(jnp.bfloat16)
    picked = jnp.dot(first, prev_ref[...], preferred_element_type=jnp.float32)
    picked = picked + jnp.dot(second, own_ref[...], preferred_element_type=jnp.float32)
    o_ref[...] = picked.astype(jnp.bfloat16)


def local(states, lengths, moved, norm_gain, qkv_weight, qkv_bias):
    yl, c = lax.axis_index("yl"), lax.axis_index("c")
    dp = lax.axis_index(DP)
    samples = lengths.shape[1]
    bf = lambda *shape: jax.ShapeDtypeStruct(shape, jnp.bfloat16)

    sent = call(reorder_kernel, bf(NX, ROWS, 128), (yl.reshape(1), states), 1, 2 * 256 * 512 * 512, 1 << 20)
    mine = lax.all_to_all(sent, "x", 0, 0, tiled=True).reshape(1, NX * ROWS, 128)
    spread = lax.all_to_all(jnp.broadcast_to(mine, (NYH, NX * ROWS, 128)), "yh", 0, 0, tiled=True)
    gain = lax.dynamic_slice_in_dim(norm_gain, dp * WROWS, WROWS, 0).astype(jnp.float32)
    scaled = (qkv_weight.astype(jnp.float32) * gain[:, None]).astype(jnp.bfloat16)
    scaled, sent_first = lax.optimization_barrier((scaled, mine))
    wown = lax.all_gather(scaled, "z", axis=0, tiled=True)
    spread, wown = lax.optimization_barrier((spread, wown))
    other = lax.ppermute(spread, "c", [(0, 1), (1, 0)])

    row_ids = jnp.arange(ROWS, dtype=jnp.int32)
    lens = lengths[0]
    starts = jnp.cumsum(lens) - lens
    begin = jnp.max(jnp.where(starts[None, :] <= row_ids[:, None], starts[None, :], 0), axis=1)
    positions = (row_ids - begin).astype(jnp.float32)
    inv_freq = ROPE_BASE ** (-(2.0 * jnp.arange(HEAD // 2, dtype=jnp.float32)) / HEAD)
    angles = positions[:, None] * inv_freq[None, :]
    cos, sin = jnp.cos(angles), jnp.sin(angles)
    cos = jnp.concatenate([cos, cos], axis=1)
    sin = jnp.concatenate([-sin, sin], axis=1)
    moving = jnp.arange(samples, dtype=jnp.int32) >= samples - moved[0]
    tail = jnp.sum(jnp.where(moving, lens, 0)).reshape(1)
    ndp = NZ * NYL * NX
    shift = [(i, i + 1) for i in range(ndp - 1)]
    incoming = lax.ppermute(tail, DP, shift)

    squares = jnp.sum(jnp.square(spread.astype(jnp.float32)), axis=(0, 2)) + jnp.sum(
        jnp.square(other.astype(jnp.float32)), axis=(0, 2)
    )
    squares = jnp.sum(lax.all_to_all(squares.reshape(NX, ROWS), "x", 0, 0, tiled=True), axis=0)
    scale = lax.rsqrt(squares / (NZ * NYL * NX * WROWS) + EPSILON).reshape(ROWS, 1)

    half = qkv_weight.shape[1] // 2
    parts = []
    for n in range(2):
        own = wown[:, n * half : (n + 1) * half]
        oth = lax.ppermute(own, "yl", [(0, 1), (1, 0)])
        partial = call(
            matmul_kernel,
            bf(NX, ROWS, half),
            (c.reshape(1), spread, other, own, oth),
            1,
            2 * NX * ROWS * 1024 * half,
            4 << 20,
            scratch=[pltpu.VMEM((1024, half), jnp.bfloat16)],
        )
        parts.append(lax.all_to_all(partial, "x", 0, 0, tiled=True))
    bias = qkv_bias.astype(jnp.float32)[None, :]
    context = call(
        attend_kernel, bf(ROWS, PER * HEAD), (lens, *parts, scale, bias, cos, sin), 1, 4 * 4 * ROWS * ROWS * HEAD, 3 << 20
    )
    previous = lax.ppermute(context, DP, shift)
    counts = jnp.concatenate([incoming, tail])
    return call(
        pack_kernel, bf(2 * ROWS, PER * HEAD), (counts, previous, context), 1, 4 * 512 * 256 * 512, 1 << 20
    )


def solution(mesh):
    fine = Mesh(mesh.devices.reshape(NZ, NYL, NX, NYH, NC), DP + TP)
    return jax.shard_map(
        local,
        mesh=fine,
        in_specs=(P(DP, TP), P(DP, None), P(DP), P(), P(DP, TP), P(TP)),
        out_specs=P(DP, TP),
        check_vma=False,
    )
```

```python
import jax
import jax.numpy as jnp
from jax import lax
from jax.experimental import pallas as pl
from jax.experimental.pallas import tpu as pltpu
from jax.sharding import Mesh
from jax.sharding import PartitionSpec as P

HEADS = 32
KV = 8
HEAD = 128
PER = HEADS // KV
EPSILON = 1e-06
ROPE_BASE = 1000000.0

NZ, NYL, NX, NYH, NC = 16, 2, 4, 4, 2
DP = ("z", "yl", "x")
TP = ("yh", "c")
WROWS = 32
ROWS = 256
VMEM = 32 << 20


def call(kernel, out_shape, args, scalars=0, flops=0, nbytes=0, scratch=()):
    smem = pl.BlockSpec(memory_space=pltpu.SMEM)
    vmem = pl.BlockSpec(memory_space=pltpu.VMEM)
    return pl.pallas_call(
        kernel,
        out_shape=out_shape,
        in_specs=[smem] * scalars + [vmem] * (len(args) - scalars),
        out_specs=vmem if not isinstance(out_shape, (list, tuple)) else [vmem] * len(out_shape),
        scratch_shapes=list(scratch),
        compiler_params=pltpu.CompilerParams(vmem_limit_bytes=VMEM),
        cost_estimate=pl.CostEstimate(flops=flops, bytes_accessed=nbytes, transcendentals=0),
    )(*args)


def prepare_kernel(at_ref, s_ref, w_ref, gain_ref, o_ref, ow_ref):
    yl, dp = at_ref[0], at_ref[1]
    feature = lax.broadcasted_iota(jnp.int32, (WROWS, gain_ref.shape[1]), 1)
    row = lax.broadcasted_iota(jnp.int32, (WROWS, gain_ref.shape[1]), 0)
    gain = jnp.where(feature == dp * WROWS + row, gain_ref[...].astype(jnp.float32), 0.0)
    gain = jnp.sum(gain, axis=1, keepdims=True)
    ow_ref[...] = (w_ref[...].astype(jnp.float32) * gain).astype(jnp.bfloat16)
    source = lax.broadcasted_iota(jnp.int32, (512, 128), 0)
    r = lax.broadcasted_iota(jnp.int32, (512, 128), 1)
    rel, zz, k = lax.shift_right_logical(r, 6), lax.shift_right_logical(r, 5) & 1, r & 31
    base = zz * 256 + (rel ^ yl) * 128 + k
    for x in range(NX):
        perm = (source == base + x * 32).astype(jnp.bfloat16)
        picked = jnp.dot(s_ref[...], perm, preferred_element_type=jnp.float32).astype(jnp.bfloat16)
        for yh in range(NYH):
            o_ref[yh, x] = picked


def matmul_kernel(c_ref, own_ref, oth0_ref, oth1_ref, wown_ref, woth_ref, o_ref, w_ref):
    c = c_ref[0]
    for rel in range(NC):
        for yh in range(NYH):
            row = pl.multiple_of((yh * 4 + (c ^ rel) * 2) * WROWS, 64)
            at = (rel * NYH + yh) * 128
            w_ref[at : at + 64] = wown_ref[pl.ds(row, 64)]
            w_ref[at + 64 : at + 128] = woth_ref[pl.ds(row, 64)]

    for n, oth_ref in enumerate((oth0_ref, oth1_ref)):
        for k in range(2):
            g = n * 2 + k
            x = jnp.concatenate([own_ref[g, yh] for yh in range(NYH)] + [oth_ref[k, yh] for yh in range(NYH)], axis=1)
            o_ref[g] = jnp.dot(x, w_ref[...], preferred_element_type=jnp.float32).astype(jnp.bfloat16)


def attend_kernel(len_ref, p_ref, r_ref, bias_ref, cos_ref, sin_ref, o_ref):
    s1 = len_ref[0]
    s2 = s1 + len_ref[1]
    s3 = s2 + len_ref[2]
    i = lax.broadcasted_iota(jnp.int32, (ROWS, ROWS), 0)
    j = lax.broadcasted_iota(jnp.int32, (ROWS, ROWS), 1)
    start = jnp.where(i >= s3, s3, jnp.where(i >= s2, s2, jnp.where(i >= s1, s1, 0)))
    allowed = (j >= start) & (j <= i)
    r = r_ref[...]
    cos, sin = cos_ref[...], sin_ref[...]

    def head(n):
        at = n * HEAD
        total = p_ref[0, :, at : at + HEAD].astype(jnp.float32)
        for k in range(1, NX):
            total = total + p_ref[k, :, at : at + HEAD].astype(jnp.float32)
        return total * r + bias_ref[:, n * HEAD : (n + 1) * HEAD]

    def rotate(v):
        return (v * cos + pltpu.roll(v, HEAD // 2, 1) * sin).astype(jnp.bfloat16)

    key = rotate(head(PER))
    value = head(PER + 1).astype(jnp.bfloat16)
    for h in range(PER):
        query = rotate(head(h))
        scores = lax.dot_general(query, key, (((1,), (1,)), ((), ())), preferred_element_type=jnp.float32)
        scores = jnp.where(allowed, scores * HEAD ** (-0.5), -1e30)
        e = jnp.exp(scores - jnp.max(scores, axis=1, keepdims=True))
        weights = (e / jnp.sum(e, axis=1, keepdims=True)).astype(jnp.bfloat16)
        o_ref[:, h * HEAD : (h + 1) * HEAD] = jnp.dot(
            weights, value, preferred_element_type=jnp.float32
        ).astype(jnp.bfloat16)


def pack_kernel(n_ref, prev_ref, own_ref, o_ref):
    incoming, tail = n_ref[0], n_ref[1]
    slot = lax.broadcasted_iota(jnp.int32, (2 * ROWS, ROWS), 0)
    row = lax.broadcasted_iota(jnp.int32, (2 * ROWS, ROWS), 1)
    first = ((slot < incoming) & (row == slot + (ROWS - incoming))).astype(jnp.bfloat16)
    second = ((row == slot - incoming) & (row < ROWS - tail)).astype(jnp.bfloat16)
    picked = jnp.dot(first, prev_ref[...], preferred_element_type=jnp.float32)
    picked = picked + jnp.dot(second, own_ref[...], preferred_element_type=jnp.float32)
    o_ref[...] = picked.astype(jnp.bfloat16)


def local(states, lengths, moved, norm_gain, qkv_weight, qkv_bias):
    yl, c = lax.axis_index("yl"), lax.axis_index("c")
    dp = lax.axis_index(DP)
    bf = lambda *shape: jax.ShapeDtypeStruct(shape, jnp.bfloat16)

    columns = qkv_weight.shape[1]
    sent, scaled = call(
        prepare_kernel,
        (bf(NYH, NX, ROWS, 128), bf(WROWS, columns)),
        (jnp.stack([yl, dp]), states, qkv_weight, norm_gain.reshape(1, -1)),
        1,
        2 * 256 * 512 * 512,
        1 << 20,
    )
    raw = lax.all_to_all(sent, "yh", 0, 0, tiled=True)
    wown = lax.all_gather(scaled, "z", axis=0, tiled=True)
    raw, wown, lens_early = lax.optimization_barrier((raw, wown, lengths))

    woth = lax.ppermute(wown, "yl", [(0, 1), (1, 0)])
    spread = lax.all_to_all(raw.transpose(1, 0, 2, 3), "x", 0, 0, tiled=True)
    others = [lax.ppermute(spread[n * 2 : n * 2 + 2], "c", [(0, 1), (1, 0)]) for n in range(2)]

    lens = lens_early[0]
    ids = jnp.arange(ROWS, dtype=jnp.int32)
    s1 = lens[0]
    s2 = s1 + lens[1]
    s3 = s2 + lens[2]
    begin = jnp.where(ids >= s3, s3, jnp.where(ids >= s2, s2, jnp.where(ids >= s1, s1, 0)))
    positions = (ids - begin).astype(jnp.float32)
    inv_freq = ROPE_BASE ** (-(2.0 * jnp.arange(HEAD // 2, dtype=jnp.float32)) / HEAD)
    angles = positions[:, None] * inv_freq[None, :]
    cos, sin = jnp.cos(angles), jnp.sin(angles)
    cos = jnp.concatenate([cos, cos], axis=1)
    sin = jnp.concatenate([-sin, sin], axis=1)
    bias = qkv_bias.astype(jnp.float32)[None, :]
    woth, cos, sin, bias = lax.optimization_barrier((woth, cos, sin, bias))

    partial = call(
        matmul_kernel,
        bf(NX, ROWS, columns),
        (c.reshape(1), spread, *others, wown, woth),
        1,
        2 * NX * ROWS * 1024 * columns,
        6 << 20,
        scratch=[pltpu.VMEM((1024, columns), jnp.bfloat16)],
    )
    partial, raw, lengths, moved = lax.optimization_barrier((partial, raw, lengths, moved))
    summed = lax.all_to_all(partial, "x", 0, 0, tiled=True)

    squares = jnp.sum(jnp.square(raw.astype(jnp.float32)), axis=(0, 1, 3))
    squares = squares + lax.ppermute(squares, "c", [(0, 1), (1, 0)])
    scale = lax.rsqrt(squares / (NZ * NYL * NX * WROWS) + EPSILON).reshape(ROWS, 1)
    samples = lengths.shape[1]
    moving = jnp.arange(samples, dtype=jnp.int32) >= samples - moved[0]
    tail = jnp.sum(jnp.where(moving, lengths[0], 0)).reshape(1)
    shift = [(i, i + 1) for i in range(NZ * NYL * NX - 1)]
    counts = jnp.concatenate([lax.ppermute(tail, DP, shift), tail])
    summed, counts, scale = lax.optimization_barrier((summed, counts, scale))

    context = call(
        attend_kernel, bf(ROWS, PER * HEAD), (lens, summed, scale, bias, cos, sin), 1, 4 * 4 * ROWS * ROWS * HEAD, 3 << 20
    )
    previous = lax.ppermute(context, DP, shift)
    return call(
        pack_kernel, bf(2 * ROWS, PER * HEAD), (counts, previous, context), 1, 4 * 512 * 256 * 512, 1 << 20
    )


def solution(mesh):
    fine = Mesh(mesh.devices.reshape(NZ, NYL, NX, NYH, NC), DP + TP)
    return jax.shard_map(
        local,
        mesh=fine,
        in_specs=(P(DP, TP), P(DP, None), P(DP), P(), P(DP, TP), P(TP)),
        out_specs=P(DP, TP),
        check_vma=False,
    )
```

```python
import jax
import jax.numpy as jnp
from jax import lax
from jax.experimental import pallas as pl
from jax.experimental.pallas import tpu as pltpu
from jax.sharding import Mesh
from jax.sharding import PartitionSpec as P

HEADS = 32
KV = 8
HEAD = 128
PER = HEADS // KV
EPSILON = 1e-06
ROPE_BASE = 1000000.0

NZ, NYL, NX, NYH, NC = 16, 2, 4, 4, 2
DP = ("z", "yl", "x")
TP = ("yh", "c")
WROWS = 32
ROWS = 256
SAMPLES = 4
EXTRA = 16
VMEM = 32 << 20


def call(kernel, out_shape, args, scalars=0, hbm=0, flops=0, nbytes=0, scratch=(), vmem_bytes=VMEM):
    smem = pl.BlockSpec(memory_space=pltpu.SMEM)
    vmem = pl.BlockSpec(memory_space=pltpu.VMEM)
    far = pl.BlockSpec(memory_space=pltpu.HBM)
    return pl.pallas_call(
        kernel,
        out_shape=out_shape,
        in_specs=[smem] * scalars + [far] * hbm + [vmem] * (len(args) - scalars - hbm),
        out_specs=[far] * len(out_shape) if isinstance(out_shape, list) else vmem,
        scratch_shapes=list(scratch),
        compiler_params=pltpu.CompilerParams(vmem_limit_bytes=vmem_bytes),
        cost_estimate=pl.CostEstimate(flops=flops, bytes_accessed=nbytes, transcendentals=0),
    )(*args)


def prepare_kernel(at_ref, s_hbm, w_hbm, gain_ref, o_hbm, ow_hbm, s_ref, w_ref, o_ref, sems):
    load_s = pltpu.make_async_copy(s_hbm, s_ref, sems.at[0])
    load_w = pltpu.make_async_copy(w_hbm, w_ref, sems.at[1])
    load_s.start()
    load_w.start()
    yl, dp = at_ref[0], at_ref[1]
    lines = gain_ref.shape[0]
    line = lax.broadcasted_iota(jnp.int32, (lines, 128), 0)
    gain = jnp.where(line == lax.shift_right_logical(dp, 2), gain_ref[...].astype(jnp.float32), 0.0)
    gain = jnp.sum(gain, axis=0, keepdims=True)
    row = lax.broadcasted_iota(jnp.int32, (WROWS, 128), 0)
    lane = lax.broadcasted_iota(jnp.int32, (WROWS, 128), 1)
    gain = jnp.sum(jnp.where(lane == (dp & 3) * WROWS + row, gain, 0.0), axis=1, keepdims=True)
    source = lax.broadcasted_iota(jnp.int32, (512, 128), 0)
    r = lax.broadcasted_iota(jnp.int32, (512, 128), 1)
    rel, zz, k = lax.shift_right_logical(r, 6), lax.shift_right_logical(r, 5) & 1, r & 31
    base = zz * 256 + (rel ^ yl) * 128 + k
    load_s.wait()
    stores = []
    for x in range(NX):
        perm = (source == base + x * 32).astype(jnp.bfloat16)
        o_ref[x] = jnp.dot(s_ref[...], perm, preferred_element_type=jnp.float32).astype(jnp.bfloat16)
        for yh in range(NYH):
            copy = pltpu.make_async_copy(o_ref.at[x], o_hbm.at[yh, x], sems.at[3 + x * NYH + yh])
            copy.start()
            stores.append(copy)
    load_w.wait()
    w_ref[...] = (w_ref[...].astype(jnp.float32) * gain).astype(jnp.bfloat16)
    copy = pltpu.make_async_copy(w_ref, ow_hbm, sems.at[2])
    copy.start()
    stores.append(copy)
    for copy in stores:
        copy.wait()


def matmul_kernel(c_ref, own_ref, oth0_ref, oth1_ref, wown_ref, woth_ref, o_ref, w_ref):
    c = c_ref[0]
    for rel in range(NC):
        for yh in range(NYH):
            row = pl.multiple_of((yh * 4 + (c ^ rel) * 2) * WROWS, 64)
            at = (rel * NYH + yh) * 128
            w_ref[at : at + 64] = wown_ref[pl.ds(row, 64)]
            w_ref[at + 64 : at + 128] = woth_ref[pl.ds(row, 64)]

    for n, oth_ref in enumerate((oth0_ref, oth1_ref)):
        for k in range(2):
            g = n * 2 + k
            x = jnp.concatenate([own_ref[g, yh] for yh in range(NYH)] + [oth_ref[k, yh] for yh in range(NYH)], axis=1)
            o_ref[g] = jnp.dot(x, w_ref[...], preferred_element_type=jnp.float32).astype(jnp.bfloat16)


def tail_of(lens, moved):
    return sum(jnp.where(n >= SAMPLES - moved, lens[n], 0) for n in range(SAMPLES))


def attend_kernel(len_ref, moved_ref, p_ref, sq_ref, sq2_ref, bias_ref, cos_ref, sin_ref, o_ref):
    s1 = len_ref[0]
    s2 = s1 + len_ref[1]
    s3 = s2 + len_ref[2]
    i = lax.broadcasted_iota(jnp.int32, (ROWS, ROWS), 0)
    j = lax.broadcasted_iota(jnp.int32, (ROWS, ROWS), 1)
    start = jnp.where(i >= s3, s3, jnp.where(i >= s2, s2, jnp.where(i >= s1, s1, 0)))
    allowed = (j >= start) & (j <= i)
    r = lax.rsqrt((sq_ref[...] + sq2_ref[...]) * (1.0 / (NZ * NYL * NX * WROWS)) + EPSILON)
    r = jnp.sum(jnp.where(i == j, r, 0.0), axis=1, keepdims=True)
    cos, sin = cos_ref[...], sin_ref[...]

    def head(n):
        at = n * HEAD
        total = p_ref[0, :, at : at + HEAD].astype(jnp.float32)
        for k in range(1, NX):
            total = total + p_ref[k, :, at : at + HEAD].astype(jnp.float32)
        return total * r + bias_ref[:, n * HEAD : (n + 1) * HEAD]

    def rotate(v):
        return (v * cos + pltpu.roll(v, HEAD // 2, 1) * sin).astype(jnp.bfloat16)

    key = rotate(head(PER))
    value = head(PER + 1).astype(jnp.bfloat16)
    for h in range(PER):
        query = rotate(head(h))
        scores = lax.dot_general(query, key, (((1,), (1,)), ((), ())), preferred_element_type=jnp.float32)
        scores = jnp.where(allowed, scores * HEAD ** (-0.5), -1e30)
        e = jnp.exp(scores - jnp.max(scores, axis=1, keepdims=True))
        weights = (e / jnp.sum(e, axis=1, keepdims=True)).astype(jnp.bfloat16)
        o_ref[:ROWS, h * HEAD : (h + 1) * HEAD] = jnp.dot(
            weights, value, preferred_element_type=jnp.float32
        ).astype(jnp.bfloat16)
    tail = tail_of(len_ref, moved_ref[0]).astype(jnp.float32)
    o_ref[ROWS:] = jnp.full((EXTRA, PER * HEAD), tail, jnp.float32).astype(jnp.bfloat16)


def pack_kernel(len_ref, moved_ref, prev_ref, own_ref, o_ref):
    tail = tail_of(len_ref, moved_ref[0])
    incoming = prev_ref[ROWS:, :HEAD].astype(jnp.float32)[:1, :1].astype(jnp.int32)
    slot = lax.broadcasted_iota(jnp.int32, (2 * ROWS, ROWS), 0)
    row = lax.broadcasted_iota(jnp.int32, (2 * ROWS, ROWS), 1)
    first = ((slot < incoming) & (row == slot + (ROWS - incoming))).astype(jnp.bfloat16)
    second = ((row == slot - incoming) & (row < ROWS - tail)).astype(jnp.bfloat16)
    picked = jnp.dot(first, prev_ref[:ROWS], preferred_element_type=jnp.float32)
    picked = picked + jnp.dot(second, own_ref[:ROWS], preferred_element_type=jnp.float32)
    o_ref[...] = picked.astype(jnp.bfloat16)


def local(states, lengths, moved, norm_gain, qkv_weight, qkv_bias):
    yl, c = lax.axis_index("yl"), lax.axis_index("c")
    dp = lax.axis_index(DP)
    bf = lambda *shape: jax.ShapeDtypeStruct(shape, jnp.bfloat16)

    columns = qkv_weight.shape[1]
    sent, scaled = call(
        prepare_kernel,
        [bf(NYH, NX, ROWS, 128), bf(WROWS, columns)],
        (jnp.stack([yl, dp]), states, qkv_weight, norm_gain.reshape(-1, 128)),
        1,
        2,
        flops=2 * 256 * 512 * 512,
        nbytes=1 << 20,
        scratch=[
            pltpu.VMEM((ROWS, 512), jnp.bfloat16),
            pltpu.VMEM((WROWS, columns), jnp.bfloat16),
            pltpu.VMEM((NX, ROWS, 128), jnp.bfloat16),
            pltpu.SemaphoreType.DMA((3 + NX * NYH,)),
        ],
        vmem_bytes=60 << 20,
    )
    raw = lax.all_to_all(sent, "yh", 0, 0, tiled=True)
    wown = lax.all_gather(scaled, "z", axis=0, tiled=True)
    raw, wown, lengths, moved, qkv_bias = lax.optimization_barrier((raw, wown, lengths, moved, qkv_bias))

    woth = lax.ppermute(wown, "yl", [(0, 1), (1, 0)])
    spread = lax.all_to_all(raw.transpose(1, 0, 2, 3), "x", 0, 0, tiled=True)

    squares = jnp.sum(jnp.square(raw.astype(jnp.float32)), axis=(0, 1, 3))
    lens = lengths[0]
    ids = jnp.arange(ROWS, dtype=jnp.int32)
    starts = [jnp.sum(lens[:n]) for n in range(SAMPLES)]
    begin = jnp.zeros_like(ids)
    for n in range(1, SAMPLES):
        begin = jnp.where(ids >= starts[n], starts[n], begin)
    positions = (ids - begin).astype(jnp.float32)
    inv_freq = ROPE_BASE ** (-(2.0 * jnp.arange(HEAD // 2, dtype=jnp.float32)) / HEAD)
    angles = positions[:, None] * inv_freq[None, :]
    cos, sin = jnp.cos(angles), jnp.sin(angles)
    cos = jnp.concatenate([cos, cos], axis=1)
    sin = jnp.concatenate([-sin, sin], axis=1)
    bias = qkv_bias.astype(jnp.float32)[None, :]
    spread, squares, bias, cos, sin = lax.optimization_barrier((spread, squares, bias, cos, sin))
    others = [lax.ppermute(spread[n * 2 : n * 2 + 2], "c", [(0, 1), (1, 0)]) for n in range(2)]

    partial = call(
        matmul_kernel,
        bf(NX, ROWS, columns),
        (c.reshape(1), spread, *others, wown, woth),
        1,
        flops=2 * NX * ROWS * 1024 * columns,
        nbytes=6 << 20,
        scratch=[pltpu.VMEM((1024, columns), jnp.bfloat16)],
    )
    partial, squares = lax.optimization_barrier((partial, squares))
    summed = lax.all_to_all(partial, "x", 0, 0, tiled=True)

    squares2 = lax.ppermute(squares, "c", [(0, 1), (1, 0)])
    context = call(
        attend_kernel,
        bf(ROWS + EXTRA, PER * HEAD),
        (lens, moved, summed, squares.reshape(1, ROWS), squares2.reshape(1, ROWS), bias, cos, sin),
        2,
        flops=4 * 4 * ROWS * ROWS * HEAD,
        nbytes=3 << 20,
    )
    previous = lax.ppermute(context, DP, [(i, i + 1) for i in range(NZ * NYL * NX - 1)])
    return call(
        pack_kernel,
        bf(2 * ROWS, PER * HEAD),
        (lens, moved, previous, context),
        2,
        flops=4 * 512 * 256 * 512,
        nbytes=1 << 20,
    )


def solution(mesh):
    fine = Mesh(mesh.devices.reshape(NZ, NYL, NX, NYH, NC), DP + TP)
    return jax.shard_map(
        local,
        mesh=fine,
        in_specs=(P(DP, TP), P(DP, None), P(DP), P(), P(DP, TP), P(TP)),
        out_specs=P(DP, TP),
        check_vma=False,
    )
```

```python
import jax
import jax.numpy as jnp
from jax import lax
from jax.experimental import pallas as pl
from jax.experimental.pallas import tpu as pltpu
from jax.sharding import Mesh
from jax.sharding import PartitionSpec as P

HEADS = 32
KV = 8
HEAD = 128
PER = HEADS // KV
EPSILON = 1e-06
ROPE_BASE = 1000000.0

NZ, NYL, NX, NYH, NC = 16, 2, 4, 4, 2
DP = ("z", "yl", "x")
TP = ("yh", "c")
WROWS = 32
ROWS = 256
SAMPLES = 4
EXTRA = 16
NEAR = (1, 3, 0)
VMEM = 16 << 20


def call(kernel, out_shape, args, scalars=0, hbm=0, flops=0, nbytes=0, scratch=(), vmem_bytes=VMEM):
    smem = pl.BlockSpec(memory_space=pltpu.SMEM)
    vmem = pl.BlockSpec(memory_space=pltpu.VMEM)
    far = pl.BlockSpec(memory_space=pltpu.HBM)
    return pl.pallas_call(
        kernel,
        out_shape=out_shape,
        in_specs=[smem] * scalars + [far] * hbm + [vmem] * (len(args) - scalars - hbm),
        out_specs=[far] * len(out_shape) if isinstance(out_shape, list) else jax.tree.map(lambda _: vmem, out_shape),
        scratch_shapes=list(scratch),
        compiler_params=pltpu.CompilerParams(vmem_limit_bytes=vmem_bytes),
        cost_estimate=pl.CostEstimate(flops=flops, bytes_accessed=nbytes, transcendentals=0),
    )(*args)


def prepare_kernel(at_ref, s_hbm, w_hbm, gain_ref, o_hbm, ow_hbm, s_ref, w_ref, o_ref, sems):
    load_s = pltpu.make_async_copy(s_hbm, s_ref, sems.at[0])
    load_w = pltpu.make_async_copy(w_hbm, w_ref, sems.at[1])
    load_s.start()
    load_w.start()
    yl, dp = at_ref[0], at_ref[1]
    lines = gain_ref.shape[0]
    line = lax.broadcasted_iota(jnp.int32, (lines, 128), 0)
    gain = jnp.where(line == lax.shift_right_logical(dp, 2), gain_ref[...].astype(jnp.float32), 0.0)
    gain = jnp.sum(gain, axis=0, keepdims=True)
    row = lax.broadcasted_iota(jnp.int32, (WROWS, 128), 0)
    lane = lax.broadcasted_iota(jnp.int32, (WROWS, 128), 1)
    gain = jnp.sum(jnp.where(lane == (dp & 3) * WROWS + row, gain, 0.0), axis=1, keepdims=True)
    source = lax.broadcasted_iota(jnp.int32, (512, 128), 0)
    r = lax.broadcasted_iota(jnp.int32, (512, 128), 1)
    rel, zz, k = lax.shift_right_logical(r, 6), lax.shift_right_logical(r, 5) & 1, r & 31
    base = zz * 256 + (rel ^ yl) * 128 + k
    load_s.wait()
    stores = []
    for x in range(NX):
        perm = (source == base + x * 32).astype(jnp.bfloat16)
        o_ref[x] = jnp.dot(s_ref[...], perm, preferred_element_type=jnp.float32).astype(jnp.bfloat16)
        for yh in range(NYH):
            copy = pltpu.make_async_copy(o_ref.at[x], o_hbm.at[yh, x], sems.at[3 + x * NYH + yh])
            copy.start()
            stores.append(copy)
    load_w.wait()
    w_ref[...] = (w_ref[...].astype(jnp.float32) * gain).astype(jnp.bfloat16)
    copy = pltpu.make_async_copy(w_ref, ow_hbm, sems.at[2])
    copy.start()
    stores.append(copy)
    for copy in stores:
        copy.wait()


def first_kernel(at_ref, own_ref, oth0_ref, oth1_ref, wown_ref, woth_ref, o_ref, w_ref, x_ref):
    far, c = at_ref[0], at_ref[1]
    for rel in range(NC):
        for yh in range(NYH):
            row = pl.multiple_of((yh * 4 + (c ^ rel) * 2) * WROWS, 64)
            at = (rel * NYH + yh) * 128
            w_ref[at : at + 64] = wown_ref[pl.ds(row, 64)]
            w_ref[at + 64 : at + 128] = woth_ref[pl.ds(row, 64)]
    half = NYH // 2

    def states(g):
        return jnp.concatenate(
            [own_ref[g, yh] for yh in range(NYH)]
            + [oth0_ref[g, yh] for yh in range(half)]
            + [oth1_ref[g, yh] for yh in range(half)],
            axis=1,
        )

    o_ref[...] = jnp.dot(states(far), w_ref[...], preferred_element_type=jnp.float32).astype(jnp.bfloat16)
    for n, step in enumerate(NEAR):
        x_ref[n] = states((far + 2 + step) & 3)


def second_kernel(x_ref, w_ref, o1_ref, o3_ref, own_ref):
    for n, ref in enumerate((o1_ref, o3_ref, own_ref)):
        ref[...] = jnp.dot(x_ref[n], w_ref[...], preferred_element_type=jnp.float32).astype(ref.dtype)


def tail_of(lens, moved):
    return sum(jnp.where(n >= SAMPLES - moved, lens[n], 0) for n in range(SAMPLES))


def attend_kernel(len_ref, moved_ref, p0_ref, p1_ref, p2_ref, sq_ref, sq2_ref, bias_ref, cos_ref, sin_ref, o_ref):
    s1 = len_ref[0]
    s2 = s1 + len_ref[1]
    s3 = s2 + len_ref[2]
    i = lax.broadcasted_iota(jnp.int32, (ROWS, ROWS), 0)
    j = lax.broadcasted_iota(jnp.int32, (ROWS, ROWS), 1)
    start = jnp.where(i >= s3, s3, jnp.where(i >= s2, s2, jnp.where(i >= s1, s1, 0)))
    allowed = (j >= start) & (j <= i)
    r = lax.rsqrt((sq_ref[...] + sq2_ref[...]) * (1.0 / (NZ * NYL * NX * WROWS)) + EPSILON)
    r = jnp.sum(jnp.where(i == j, r, 0.0), axis=1, keepdims=True)
    cos, sin = cos_ref[...], sin_ref[...]

    def head(n):
        at = n * HEAD
        total = p0_ref[:, at : at + HEAD]
        for ref in (p1_ref, p2_ref):
            total = total + ref[:, at : at + HEAD].astype(jnp.float32)
        return total * r + bias_ref[:, n * HEAD : (n + 1) * HEAD]

    def rotate(v):
        return (v * cos + pltpu.roll(v, HEAD // 2, 1) * sin).astype(jnp.bfloat16)

    key = rotate(head(PER))
    value = head(PER + 1).astype(jnp.bfloat16)
    for h in range(PER):
        query = rotate(head(h))
        scores = lax.dot_general(query, key, (((1,), (1,)), ((), ())), preferred_element_type=jnp.float32)
        scores = jnp.where(allowed, scores * HEAD ** (-0.5), -1e30)
        e = jnp.exp(scores - jnp.max(scores, axis=1, keepdims=True))
        weights = (e / jnp.sum(e, axis=1, keepdims=True)).astype(jnp.bfloat16)
        o_ref[:ROWS, h * HEAD : (h + 1) * HEAD] = jnp.dot(
            weights, value, preferred_element_type=jnp.float32
        ).astype(jnp.bfloat16)
    tail = tail_of(len_ref, moved_ref[0]).astype(jnp.float32)
    o_ref[ROWS:] = jnp.full((EXTRA, PER * HEAD), tail, jnp.float32).astype(jnp.bfloat16)


def pack_kernel(len_ref, moved_ref, prev_ref, own_ref, o_ref):
    tail = tail_of(len_ref, moved_ref[0])
    incoming = prev_ref[ROWS:, :HEAD].astype(jnp.float32)[:1, :1].astype(jnp.int32)
    slot = lax.broadcasted_iota(jnp.int32, (2 * ROWS, ROWS), 0)
    row = lax.broadcasted_iota(jnp.int32, (2 * ROWS, ROWS), 1)
    first = ((slot < incoming) & (row == slot + (ROWS - incoming))).astype(jnp.bfloat16)
    second = ((row == slot - incoming) & (row < ROWS - tail)).astype(jnp.bfloat16)
    picked = jnp.dot(first, prev_ref[:ROWS], preferred_element_type=jnp.float32)
    picked = picked + jnp.dot(second, own_ref[:ROWS], preferred_element_type=jnp.float32)
    o_ref[...] = picked.astype(jnp.bfloat16)


def local(states, lengths, moved, norm_gain, qkv_weight, qkv_bias):
    yl, c = lax.axis_index("yl"), lax.axis_index("c")
    dp = lax.axis_index(DP)
    bf = lambda *shape: jax.ShapeDtypeStruct(shape, jnp.bfloat16)

    columns = qkv_weight.shape[1]
    sent, scaled = call(
        prepare_kernel,
        [bf(NYH, NX, ROWS, 128), bf(WROWS, columns)],
        (jnp.stack([yl, dp]), states, qkv_weight, norm_gain.reshape(-1, 128)),
        1,
        2,
        flops=2 * 256 * 512 * 512,
        nbytes=1 << 20,
        scratch=[
            pltpu.VMEM((ROWS, 512), jnp.bfloat16),
            pltpu.VMEM((WROWS, columns), jnp.bfloat16),
            pltpu.VMEM((NX, ROWS, 128), jnp.bfloat16),
            pltpu.SemaphoreType.DMA((3 + NX * NYH,)),
        ],
        vmem_bytes=60 << 20,
    )
    raw = lax.all_to_all(sent, "yh", 0, 0, tiled=True)
    wown = lax.all_gather(scaled, "z", axis=0, tiled=True)
    raw, wown, lengths, moved, qkv_bias = lax.optimization_barrier((raw, wown, lengths, moved, qkv_bias))

    woth = lax.ppermute(wown, "yl", [(0, 1), (1, 0)])
    spread = lax.all_to_all(raw.transpose(1, 0, 2, 3), "x", 0, 0, tiled=True)

    squares = jnp.sum(jnp.square(raw.astype(jnp.float32)), axis=(0, 1, 3))
    lens = lengths[0]
    ids = jnp.arange(ROWS, dtype=jnp.int32)
    starts = [jnp.sum(lens[:n]) for n in range(SAMPLES)]
    begin = jnp.zeros_like(ids)
    for n in range(1, SAMPLES):
        begin = jnp.where(ids >= starts[n], starts[n], begin)
    positions = (ids - begin).astype(jnp.float32)
    inv_freq = ROPE_BASE ** (-(2.0 * jnp.arange(HEAD // 2, dtype=jnp.float32)) / HEAD)
    angles = positions[:, None] * inv_freq[None, :]
    cos, sin = jnp.cos(angles), jnp.sin(angles)
    cos = jnp.concatenate([cos, cos], axis=1)
    sin = jnp.concatenate([-sin, sin], axis=1)
    bias = qkv_bias.astype(jnp.float32)[None, :]
    spread, squares, bias, cos, sin = lax.optimization_barrier((spread, squares, bias, cos, sin))
    others = [lax.ppermute(spread[:, n * 2 : n * 2 + 2], "c", [(0, 1), (1, 0)]) for n in range(2)]

    x = lax.axis_index("x")
    whole = lambda step, v: lax.ppermute(v, "x", [(i, (i + step) % NX) for i in range(NX)])
    flops = 2 * ROWS * 1024 * columns
    far, weights, near = call(
        first_kernel,
        (bf(ROWS, columns), bf(1024, columns), bf(3, ROWS, 1024)),
        (jnp.stack([(x + 2) & 3, c]), spread, *others, wown, woth),
        1,
        flops=flops,
        nbytes=6 << 20,
    )
    far = whole(2, far)
    right, left, own = call(
        second_kernel,
        (bf(ROWS, columns), bf(ROWS, columns), jax.ShapeDtypeStruct((ROWS, columns), jnp.float32)),
        (near, weights),
        flops=3 * flops,
        nbytes=4 << 20,
    )
    right, left = whole(1, right), whole(3, left)
    own, squares = lax.optimization_barrier((own, squares))
    own = own + far.astype(jnp.float32)
    squares2 = lax.ppermute(squares, "c", [(0, 1), (1, 0)])
    context = call(
        attend_kernel,
        bf(ROWS + EXTRA, PER * HEAD),
        (lens, moved, own, right, left, squares.reshape(1, ROWS), squares2.reshape(1, ROWS), bias, cos, sin),
        2,
        flops=4 * 4 * ROWS * ROWS * HEAD,
        nbytes=3 << 20,
    )
    previous = lax.ppermute(context, DP, [(i, i + 1) for i in range(NZ * NYL * NX - 1)])
    return call(
        pack_kernel,
        bf(2 * ROWS, PER * HEAD),
        (lens, moved, previous, context),
        2,
        flops=4 * 512 * 256 * 512,
        nbytes=1 << 20,
    )


def solution(mesh):
    fine = Mesh(mesh.devices.reshape(NZ, NYL, NX, NYH, NC), DP + TP)
    return jax.shard_map(
        local,
        mesh=fine,
        in_specs=(P(DP, TP), P(DP, None), P(DP), P(), P(DP, TP), P(TP)),
        out_specs=P(DP, TP),
        check_vma=False,
    )
```

```python
import jax
import jax.numpy as jnp
from jax import lax
from jax.experimental import pallas as pl
from jax.experimental.pallas import tpu as pltpu
from jax.sharding import Mesh
from jax.sharding import PartitionSpec as P

HEADS = 32
KV = 8
HEAD = 128
PER = HEADS // KV
EPSILON = 1e-06
ROPE_BASE = 1000000.0

NZH, NQ, NX, NYH, NC = 8, 4, 4, 4, 2
Q = ("zl", "yl")
DP = ("zh",) + Q + ("x",)
TP = ("yh", "c")
NDP = NZH * NQ * NX
WROWS = 32
ROWS = 256
SAMPLES = 4
EXTRA = 16
FULL = ROWS + EXTRA
NEAR = (1, 2, 0)
VMEM = 16 << 20


def call(kernel, out_shape, args, scalars=0, hbm=0, flops=0, nbytes=0, scratch=(), vmem_bytes=VMEM):
    smem = pl.BlockSpec(memory_space=pltpu.SMEM)
    vmem = pl.BlockSpec(memory_space=pltpu.VMEM)
    far = pl.BlockSpec(memory_space=pltpu.HBM)
    return pl.pallas_call(
        kernel,
        out_shape=out_shape,
        in_specs=[smem] * scalars + [far] * hbm + [vmem] * (len(args) - scalars - hbm),
        out_specs=[far] * len(out_shape) if isinstance(out_shape, list) else jax.tree.map(lambda _: vmem, out_shape),
        scratch_shapes=list(scratch),
        compiler_params=pltpu.CompilerParams(vmem_limit_bytes=vmem_bytes),
        cost_estimate=pl.CostEstimate(flops=flops, bytes_accessed=nbytes, transcendentals=0),
    )(*args)


def prepare_kernel(dp_ref, s_hbm, w_hbm, gain_ref, o_hbm, ow_hbm, w_ref, sems):
    copies = []
    for q in range(NQ):
        copy = pltpu.make_async_copy(s_hbm.at[:, q * 128 : (q + 1) * 128], o_hbm.at[q], sems.at[2 + q])
        copy.start()
        copies.append(copy)
    load = pltpu.make_async_copy(w_hbm, w_ref, sems.at[0])
    load.start()
    dp = dp_ref[0]
    line = lax.broadcasted_iota(jnp.int32, (gain_ref.shape[0], 128), 0)
    gain = jnp.where(line == lax.shift_right_logical(dp, 2), gain_ref[...].astype(jnp.float32), 0.0)
    gain = jnp.sum(gain, axis=0, keepdims=True)
    row = lax.broadcasted_iota(jnp.int32, (WROWS, 128), 0)
    lane = lax.broadcasted_iota(jnp.int32, (WROWS, 128), 1)
    gain = jnp.sum(jnp.where(lane == (dp & 3) * WROWS + row, gain, 0.0), axis=1, keepdims=True)
    load.wait()
    w_ref[...] = (w_ref[...].astype(jnp.float32) * gain).astype(jnp.bfloat16)
    store = pltpu.make_async_copy(w_ref, ow_hbm, sems.at[1])
    store.start()
    copies.append(store)
    for copy in copies:
        copy.wait()


def product(x, w_ref, o_ref):
    o_ref[:ROWS] = jnp.dot(x, w_ref[...], preferred_element_type=jnp.float32).astype(o_ref.dtype)
    square = jnp.square(x.astype(jnp.float32))
    high = square.astype(jnp.bfloat16)
    low = (square - high.astype(jnp.float32)).astype(jnp.bfloat16)
    ones = jnp.ones((EXTRA, x.shape[1]), jnp.bfloat16)
    lanes = (((1,), (1,)), ((), ()))
    total = lax.dot_general(ones, high, lanes, preferred_element_type=jnp.float32)
    total = total + lax.dot_general(ones, low, lanes, preferred_element_type=jnp.float32)
    rounded = total.astype(jnp.bfloat16).astype(jnp.float32)
    row = lax.broadcasted_iota(jnp.int32, total.shape, 0)
    o_ref[ROWS:, :ROWS] = jnp.where(row < EXTRA // 2, rounded, total - rounded).astype(o_ref.dtype)
    o_ref[ROWS:, ROWS:] = jnp.zeros((EXTRA, o_ref.shape[1] - ROWS), o_ref.dtype)


def first_kernel(q_ref, x_at_ref, c_ref, own_ref, *refs):
    others, weights, (o_ref, w_ref, x_ref) = refs[:NYH], refs[NYH : NYH + NX], refs[NYH + NX :]
    q, c = q_ref[0], c_ref[0]
    for step, ref in enumerate(weights):
        source = (x_at_ref[0] + (NX - step)) & 3
        for rel in range(NC):
            for yh in range(NYH):
                row = pl.multiple_of((yh * NC + (c ^ rel)) * WROWS, WROWS)
                at = pl.multiple_of((rel * NYH + yh) * 128 + source * WROWS, WROWS)
                w_ref[pl.ds(at, WROWS)] = ref[pl.ds(row, WROWS)]

    def states(r):
        rows = pl.ds(pl.multiple_of((q ^ r) * ROWS, ROWS), ROWS)
        return jnp.concatenate([own_ref[yh, rows] for yh in range(NYH)] + [ref[rows] for ref in others], axis=1)

    product(states(3), w_ref, o_ref)
    for n, r in enumerate(NEAR):
        x_ref[n] = states(r)


def second_kernel(x_ref, w_ref, o1_ref, o2_ref, own_ref):
    for n, ref in enumerate((o1_ref, o2_ref, own_ref)):
        product(x_ref[n], w_ref, ref)


def tail_of(lens, moved):
    return sum(jnp.where(n >= SAMPLES - moved, lens[n], 0) for n in range(SAMPLES))


def attend_kernel(len_ref, moved_ref, p0_ref, p1_ref, p2_ref, bias_ref, cos_ref, sin_ref, o_ref):
    s1 = len_ref[0]
    s2 = s1 + len_ref[1]
    s3 = s2 + len_ref[2]
    i = lax.broadcasted_iota(jnp.int32, (ROWS, ROWS), 0)
    j = lax.broadcasted_iota(jnp.int32, (ROWS, ROWS), 1)
    start = jnp.where(i >= s3, s3, jnp.where(i >= s2, s2, jnp.where(i >= s1, s1, 0)))
    allowed = (j >= start) & (j <= i)
    squares = jnp.zeros((1, ROWS), jnp.float32)
    for ref in (p0_ref, p1_ref, p2_ref):
        for row in (0, EXTRA // 2):
            part = ref[ROWS:, :ROWS].astype(jnp.float32)
            squares = squares + part[row : row + 1]
    r = lax.rsqrt(squares * (1.0 / (NDP * WROWS)) + EPSILON)
    r = jnp.sum(jnp.where(i == j, r, 0.0), axis=1, keepdims=True)
    cos, sin = cos_ref[...], sin_ref[...]

    def head(n):
        at = n * HEAD
        total = p0_ref[:ROWS, at : at + HEAD]
        for ref in (p1_ref, p2_ref):
            total = total + ref[:ROWS, at : at + HEAD].astype(jnp.float32)
        return total * r + bias_ref[:, n * HEAD : (n + 1) * HEAD]

    def rotate(v):
        return (v * cos + pltpu.roll(v, HEAD // 2, 1) * sin).astype(jnp.bfloat16)

    key = rotate(head(PER))
    value = head(PER + 1).astype(jnp.bfloat16)
    for h in range(PER):
        query = rotate(head(h))
        scores = lax.dot_general(query, key, (((1,), (1,)), ((), ())), preferred_element_type=jnp.float32)
        scores = jnp.where(allowed, scores * HEAD ** (-0.5), -1e30)
        e = jnp.exp(scores - jnp.max(scores, axis=1, keepdims=True))
        weights = (e / jnp.sum(e, axis=1, keepdims=True)).astype(jnp.bfloat16)
        o_ref[:ROWS, h * HEAD : (h + 1) * HEAD] = jnp.dot(
            weights, value, preferred_element_type=jnp.float32
        ).astype(jnp.bfloat16)
    tail = tail_of(len_ref, moved_ref[0]).astype(jnp.float32)
    o_ref[ROWS:] = jnp.full((EXTRA, PER * HEAD), tail, jnp.float32).astype(jnp.bfloat16)


def pack_kernel(len_ref, moved_ref, prev_ref, own_ref, o_ref):
    tail = tail_of(len_ref, moved_ref[0])
    incoming = prev_ref[ROWS:, :HEAD].astype(jnp.float32)[:1, :1].astype(jnp.int32)
    slot = lax.broadcasted_iota(jnp.int32, (2 * ROWS, ROWS), 0)
    row = lax.broadcasted_iota(jnp.int32, (2 * ROWS, ROWS), 1)
    first = ((slot < incoming) & (row == slot + (ROWS - incoming))).astype(jnp.bfloat16)
    second = ((row == slot - incoming) & (row < ROWS - tail)).astype(jnp.bfloat16)
    picked = jnp.dot(first, prev_ref[:ROWS], preferred_element_type=jnp.float32)
    picked = picked + jnp.dot(second, own_ref[:ROWS], preferred_element_type=jnp.float32)
    o_ref[...] = picked.astype(jnp.bfloat16)


def local(states, lengths, moved, norm_gain, qkv_weight, qkv_bias):
    scalar = lambda v: v.astype(jnp.int32).reshape(1)
    at = {name: scalar(lax.axis_index(name)) for name in ("x", "c")}
    at["q"], at["dp"] = scalar(lax.axis_index(Q)), scalar(lax.axis_index(DP))
    bf = lambda *shape: jax.ShapeDtypeStruct(shape, jnp.bfloat16)
    columns = qkv_weight.shape[1]

    sent, scaled = call(
        prepare_kernel,
        [bf(NQ, ROWS, 128), bf(WROWS, columns)],
        (at["dp"], states, qkv_weight, norm_gain.reshape(-1, 128)),
        1,
        2,
        nbytes=1 << 20,
        scratch=[pltpu.VMEM((WROWS, columns), jnp.bfloat16), pltpu.SemaphoreType.DMA((2 + NQ,))],
        vmem_bytes=60 << 20,
    )
    mine = lax.all_to_all(sent, Q, 0, 0, tiled=True).reshape(1, NQ * ROWS, 128)
    mine, scaled = lax.optimization_barrier((mine, scaled))
    spread = lax.all_to_all(jnp.broadcast_to(mine, (NYH, NQ * ROWS, 128)), "yh", 0, 0, tiled=True)
    held = lax.all_gather(scaled, "zh", axis=0, tiled=True)
    held, lengths_late, qkv_bias = lax.optimization_barrier((held, lengths, qkv_bias))

    send = lambda v, axis, count, to: lax.ppermute(v, axis, [(i, to(i)) for i in range(count)])
    weights = {0: held}
    for step in (2, 1, 3):
        weights[step] = send(held, "x", NX, lambda i: (i + step) % NX)

    lens = lengths_late[0]
    ids = jnp.arange(ROWS, dtype=jnp.int32)
    starts = [jnp.sum(lens[:n]) for n in range(SAMPLES)]
    begin = jnp.zeros_like(ids)
    for n in range(1, SAMPLES):
        begin = jnp.where(ids >= starts[n], starts[n], begin)
    positions = (ids - begin).astype(jnp.float32)
    inv_freq = ROPE_BASE ** (-(2.0 * jnp.arange(HEAD // 2, dtype=jnp.float32)) / HEAD)
    angles = positions[:, None] * inv_freq[None, :]
    cos, sin = jnp.cos(angles), jnp.sin(angles)
    cos = jnp.concatenate([cos, cos], axis=1)
    sin = jnp.concatenate([-sin, sin], axis=1)
    bias = qkv_bias.astype(jnp.float32)[None, :]

    spread, bias, cos, sin = lax.optimization_barrier((spread, bias, cos, sin))
    others = [send(spread[n], "c", NC, lambda i: 1 - i) for n in range(NYH)]

    flops = 2 * ROWS * 1024 * columns
    far, packed, near = call(
        first_kernel,
        (bf(FULL, columns), bf(1024, columns), bf(3, ROWS, 1024)),
        (at["q"], at["x"], at["c"], spread, *others, *[weights[step] for step in range(NX)]),
        3,
        flops=flops,
        nbytes=6 << 20,
    )
    far = send(far, Q, NQ, lambda i: i ^ 3)
    one, two, own = call(
        second_kernel,
        (bf(FULL, columns), bf(FULL, columns), jax.ShapeDtypeStruct((FULL, columns), jnp.float32)),
        (near, packed),
        flops=3 * flops,
        nbytes=4 << 20,
    )
    one, two = send(one, Q, NQ, lambda i: i ^ 1), send(two, Q, NQ, lambda i: i ^ 2)
    own = own + far.astype(jnp.float32)
    context = call(
        attend_kernel,
        bf(FULL, PER * HEAD),
        (lens, moved, own, one, two, bias, cos, sin),
        2,
        flops=4 * 4 * ROWS * ROWS * HEAD,
        nbytes=3 << 20,
    )
    previous = lax.ppermute(context, DP, [(i, i + 1) for i in range(NDP - 1)])
    return call(
        pack_kernel,
        bf(2 * ROWS, PER * HEAD),
        (lens, moved, previous, context),
        2,
        flops=4 * 512 * 256 * 512,
        nbytes=1 << 20,
    )


def solution(mesh):
    fine = Mesh(mesh.devices.reshape(NZH, 2, 2, NX, NYH, NC), DP + TP)
    return jax.shard_map(
        local,
        mesh=fine,
        in_specs=(P(DP, TP), P(DP, None), P(DP), P(), P(DP, TP), P(TP)),
        out_specs=P(DP, TP),
        check_vma=False,
    )
```

```python
import jax
import jax.numpy as jnp
from jax import lax
from jax.experimental import pallas as pl
from jax.experimental.pallas import tpu as pltpu
from jax.sharding import Mesh
from jax.sharding import PartitionSpec as P

HEADS = 32
KV = 8
HEAD = 128
PER = HEADS // KV
EPSILON = 1e-06
ROPE_BASE = 1000000.0

NZ, NYL, NX, NYH, NC = 16, 2, 4, 4, 2
DP = ("z", "yl", "x")
TP = ("yh", "c")
WROWS = 32
ROWS = 256
SAMPLES = 4
EXTRA = 16
FULL = ROWS + EXTRA
FIRST = 512
STEPS = (2, 1, 3, 0)
VMEM = 16 << 20


def call(kernel, out_shape, args, scalars=0, hbm=0, flops=0, nbytes=0, scratch=(), vmem_bytes=VMEM):
    smem = pl.BlockSpec(memory_space=pltpu.SMEM)
    vmem = pl.BlockSpec(memory_space=pltpu.VMEM)
    far = pl.BlockSpec(memory_space=pltpu.HBM)
    return pl.pallas_call(
        kernel,
        out_shape=out_shape,
        in_specs=[smem] * scalars + [far] * hbm + [vmem] * (len(args) - scalars - hbm),
        out_specs=[far] * len(out_shape) if isinstance(out_shape, list) else jax.tree.map(lambda _: vmem, out_shape),
        scratch_shapes=list(scratch),
        compiler_params=pltpu.CompilerParams(vmem_limit_bytes=vmem_bytes),
        cost_estimate=pl.CostEstimate(flops=flops, bytes_accessed=nbytes, transcendentals=0),
    )(*args)


def prepare_kernel(yl_ref, dp_ref, s_hbm, w_hbm, gain_ref, o_hbm, ow_hbm, s_ref, w_ref, o_ref, sems):
    load_s = pltpu.make_async_copy(s_hbm, s_ref, sems.at[0])
    load_w = pltpu.make_async_copy(w_hbm, w_ref, sems.at[1])
    load_s.start()
    load_w.start()
    yl, dp = yl_ref[0], dp_ref[0]
    lines = gain_ref.shape[0]
    line = lax.broadcasted_iota(jnp.int32, (lines, 128), 0)
    gain = jnp.where(line == lax.shift_right_logical(dp, 2), gain_ref[...].astype(jnp.float32), 0.0)
    gain = jnp.sum(gain, axis=0, keepdims=True)
    row = lax.broadcasted_iota(jnp.int32, (WROWS, 128), 0)
    lane = lax.broadcasted_iota(jnp.int32, (WROWS, 128), 1)
    gain = jnp.sum(jnp.where(lane == (dp & 3) * WROWS + row, gain, 0.0), axis=1, keepdims=True)
    source = lax.broadcasted_iota(jnp.int32, (512, 128), 0)
    r = lax.broadcasted_iota(jnp.int32, (512, 128), 1)
    rel, zz, k = lax.shift_right_logical(r, 6), lax.shift_right_logical(r, 5) & 1, r & 31
    base = zz * 256 + (rel ^ yl) * 128 + k
    load_w.wait()
    w_ref[...] = (w_ref[...].astype(jnp.float32) * gain).astype(jnp.bfloat16)
    copy = pltpu.make_async_copy(w_ref, ow_hbm, sems.at[2])
    copy.start()
    stores = [copy]
    load_s.wait()
    for x in range(NX):
        perm = (source == base + x * 32).astype(jnp.bfloat16)
        o_ref[x] = jnp.dot(s_ref[...], perm, preferred_element_type=jnp.float32).astype(jnp.bfloat16)
        copy = pltpu.make_async_copy(o_ref.at[x], o_hbm.at[x], sems.at[3 + x])
        copy.start()
        stores.append(copy)
    for copy in stores:
        copy.wait()


def arrange(c, wown_ref, woth_ref, w_ref):
    for rel in range(NC):
        for yh in range(NYH):
            row = pl.multiple_of((yh * 4 + (c ^ rel) * 2) * WROWS, 64)
            at = (rel * NYH + yh) * 128
            w_ref[at : at + 64] = wown_ref[pl.ds(row, 64)]
            w_ref[at + 64 : at + 128] = woth_ref[pl.ds(row, 64)]


def first_kernel(x_ref, c_ref, own_ref, oth_ref, wown_ref, woth_ref, o2_ref, o1_ref, o3_ref, o0_ref, s_ref, w_ref):
    arrange(c_ref[0], wown_ref, woth_ref, w_ref)
    for n, (step, o_ref) in enumerate(zip(STEPS, (o2_ref, o1_ref, o3_ref, o0_ref))):
        rows = pl.ds(pl.multiple_of(((x_ref[0] + step) & 3) * ROWS, ROWS), ROWS)
        x = jnp.concatenate([ref[yh, rows] for ref in (own_ref, oth_ref) for yh in range(NYH)], axis=1)
        s_ref[n] = x
        o_ref[:ROWS] = jnp.dot(x, w_ref[...], preferred_element_type=jnp.float32).astype(o_ref.dtype)
        square = jnp.square(x.astype(jnp.float32))
        high = square.astype(jnp.bfloat16)
        low = (square - high.astype(jnp.float32)).astype(jnp.bfloat16)
        ones = jnp.ones((EXTRA, x.shape[1]), jnp.bfloat16)
        lanes = (((1,), (1,)), ((), ()))
        total = lax.dot_general(ones, high, lanes, preferred_element_type=jnp.float32)
        total = total + lax.dot_general(ones, low, lanes, preferred_element_type=jnp.float32)
        rounded = total.astype(jnp.bfloat16).astype(jnp.float32)
        row = lax.broadcasted_iota(jnp.int32, total.shape, 0)
        o_ref[ROWS:, :ROWS] = jnp.where(row < EXTRA // 2, rounded, total - rounded).astype(o_ref.dtype)
        o_ref[ROWS:, ROWS:] = jnp.zeros((EXTRA, o_ref.shape[1] - ROWS), o_ref.dtype)


def second_kernel(c_ref, s_ref, wown_ref, woth_ref, o2_ref, o1_ref, o3_ref, o0_ref, w_ref):
    arrange(c_ref[0], wown_ref, woth_ref, w_ref)
    for n, o_ref in enumerate((o2_ref, o1_ref, o3_ref, o0_ref)):
        o_ref[...] = jnp.dot(s_ref[n], w_ref[...], preferred_element_type=jnp.float32).astype(o_ref.dtype)


def tail_of(lens, moved):
    return sum(jnp.where(n >= SAMPLES - moved, lens[n], 0) for n in range(SAMPLES))


def attend_kernel(len_ref, moved_ref, bias_ref, cos_ref, sin_ref, *refs):
    first, second, o_ref = refs[:NX], refs[NX : 2 * NX], refs[2 * NX]
    s1 = len_ref[0]
    s2 = s1 + len_ref[1]
    s3 = s2 + len_ref[2]
    i = lax.broadcasted_iota(jnp.int32, (ROWS, ROWS), 0)
    j = lax.broadcasted_iota(jnp.int32, (ROWS, ROWS), 1)
    start = jnp.where(i >= s3, s3, jnp.where(i >= s2, s2, jnp.where(i >= s1, s1, 0)))
    allowed = (j >= start) & (j <= i)
    squares = jnp.zeros((1, ROWS), jnp.float32)
    for ref in first:
        part = ref[ROWS:, :ROWS].astype(jnp.float32)
        squares = squares + part[:1] + part[EXTRA // 2 : EXTRA // 2 + 1]
    r = lax.rsqrt(squares * (1.0 / (NZ * NYL * NX * WROWS)) + EPSILON)
    r = jnp.sum(jnp.where(i == j, r, 0.0), axis=1, keepdims=True)
    cos, sin = cos_ref[...], sin_ref[...]

    def head(n):
        refs, at = (first, n * HEAD) if n * HEAD < FIRST else (second, n * HEAD - FIRST)
        total = refs[0][:ROWS, at : at + HEAD].astype(jnp.float32)
        for ref in refs[1:]:
            total = total + ref[:ROWS, at : at + HEAD].astype(jnp.float32)
        return total * r + bias_ref[:, n * HEAD : (n + 1) * HEAD]

    def rotate(v):
        return (v * cos + pltpu.roll(v, HEAD // 2, 1) * sin).astype(jnp.bfloat16)

    key = rotate(head(PER))
    value = head(PER + 1).astype(jnp.bfloat16)
    for h in range(PER):
        query = rotate(head(h))
        scores = lax.dot_general(query, key, (((1,), (1,)), ((), ())), preferred_element_type=jnp.float32)
        scores = jnp.where(allowed, scores * HEAD ** (-0.5), -1e30)
        e = jnp.exp(scores - jnp.max(scores, axis=1, keepdims=True))
        weights = (e / jnp.sum(e, axis=1, keepdims=True)).astype(jnp.bfloat16)
        o_ref[:ROWS, h * HEAD : (h + 1) * HEAD] = jnp.dot(
            weights, value, preferred_element_type=jnp.float32
        ).astype(jnp.bfloat16)
    tail = tail_of(len_ref, moved_ref[0]).astype(jnp.float32)
    o_ref[ROWS:] = jnp.full((EXTRA, PER * HEAD), tail, jnp.float32).astype(jnp.bfloat16)


def pack_kernel(len_ref, moved_ref, prev_ref, own_ref, o_ref):
    tail = tail_of(len_ref, moved_ref[0])
    incoming = prev_ref[ROWS:, :HEAD].astype(jnp.float32)[:1, :1].astype(jnp.int32)
    slot = lax.broadcasted_iota(jnp.int32, (2 * ROWS, ROWS), 0)
    row = lax.broadcasted_iota(jnp.int32, (2 * ROWS, ROWS), 1)
    first = ((slot < incoming) & (row == slot + (ROWS - incoming))).astype(jnp.bfloat16)
    second = ((row == slot - incoming) & (row < ROWS - tail)).astype(jnp.bfloat16)
    picked = jnp.dot(first, prev_ref[:ROWS], preferred_element_type=jnp.float32)
    picked = picked + jnp.dot(second, own_ref[:ROWS], preferred_element_type=jnp.float32)
    o_ref[...] = picked.astype(jnp.bfloat16)


def local(states, lengths, moved, norm_gain, qkv_weight, qkv_bias):
    scalar = lambda v: v.astype(jnp.int32).reshape(1)
    x, yl, c, dp = [scalar(lax.axis_index(name)) for name in ("x", "yl", "c", DP)]
    bf = lambda *shape: jax.ShapeDtypeStruct(shape, jnp.bfloat16)
    columns = qkv_weight.shape[1]

    sent, scaled = call(
        prepare_kernel,
        [bf(NX, ROWS, 128), bf(WROWS, columns)],
        (yl, dp, states, qkv_weight, norm_gain.reshape(-1, 128)),
        2,
        2,
        flops=2 * 256 * 512 * 512,
        nbytes=1 << 20,
        scratch=[
            pltpu.VMEM((ROWS, 512), jnp.bfloat16),
            pltpu.VMEM((WROWS, columns), jnp.bfloat16),
            pltpu.VMEM((NX, ROWS, 128), jnp.bfloat16),
            pltpu.SemaphoreType.DMA((3 + NX,)),
        ],
        vmem_bytes=60 << 20,
    )
    mine = lax.all_to_all(sent, "x", 0, 0, tiled=True).reshape(1, NX * ROWS, 128)
    mine, scaled = lax.optimization_barrier((mine, scaled))
    spread = lax.all_to_all(jnp.broadcast_to(mine, (NYH, NX * ROWS, 128)), "yh", 0, 0, tiled=True)
    held = lax.all_gather(scaled, "z", axis=0, tiled=True)
    spread, held, lengths, qkv_bias = lax.optimization_barrier((spread, held, lengths, qkv_bias))

    send = lambda v, axis, count, to: lax.ppermute(v, axis, [(i, to(i)) for i in range(count)])
    other = send(spread, "c", NC, lambda i: 1 - i)
    held1, held2 = held[:, :FIRST], held[:, FIRST:]
    came1 = send(held1, "yl", NYL, lambda i: 1 - i)
    came1, held2 = lax.optimization_barrier((came1, held2))
    came2 = send(held2, "yl", NYL, lambda i: 1 - i)

    lens = lengths[0]
    ids = jnp.arange(ROWS, dtype=jnp.int32)
    starts = [jnp.sum(lens[:n]) for n in range(SAMPLES)]
    begin = jnp.zeros_like(ids)
    for n in range(1, SAMPLES):
        begin = jnp.where(ids >= starts[n], starts[n], begin)
    positions = (ids - begin).astype(jnp.float32)
    inv_freq = ROPE_BASE ** (-(2.0 * jnp.arange(HEAD // 2, dtype=jnp.float32)) / HEAD)
    angles = positions[:, None] * inv_freq[None, :]
    cos, sin = jnp.cos(angles), jnp.sin(angles)
    cos = jnp.concatenate([cos, cos], axis=1)
    sin = jnp.concatenate([-sin, sin], axis=1)
    bias = qkv_bias.astype(jnp.float32)[None, :]
    came1, bias, cos, sin = lax.optimization_barrier((came1, bias, cos, sin))

    def outputs(rows, count):
        return (bf(rows, count),) * (NX - 1) + (jax.ShapeDtypeStruct((rows, count), jnp.float32),)

    def spread_x(parts):
        return [send(v, "x", NX, lambda i: (i + step) % NX) for v, step in zip(parts, STEPS[: NX - 1])] + [parts[NX - 1]]

    *parts, packed = call(
        first_kernel,
        outputs(FULL, FIRST) + (bf(NX, ROWS, 1024),),
        (x, c, spread, other, held1, came1),
        2,
        flops=2 * NX * ROWS * 1024 * FIRST,
        nbytes=6 << 20,
        scratch=[pltpu.VMEM((1024, FIRST), jnp.bfloat16)],
    )
    first = spread_x(parts)
    came2, first[0] = lax.optimization_barrier((came2, first[0]))
    parts = call(
        second_kernel,
        outputs(ROWS, columns - FIRST),
        (c, packed, held2, came2),
        1,
        flops=2 * NX * ROWS * 1024 * (columns - FIRST),
        nbytes=4 << 20,
        scratch=[pltpu.VMEM((1024, columns - FIRST), jnp.bfloat16)],
    )
    second = spread_x(parts)
    context = call(
        attend_kernel,
        bf(FULL, PER * HEAD),
        (lens, moved, bias, cos, sin, *first, *second),
        2,
        flops=4 * 4 * ROWS * ROWS * HEAD,
        nbytes=3 << 20,
    )
    previous = lax.ppermute(context, DP, [(i, i + 1) for i in range(NZ * NYL * NX - 1)])
    return call(
        pack_kernel,
        bf(2 * ROWS, PER * HEAD),
        (lens, moved, previous, context),
        2,
        flops=4 * 512 * 256 * 512,
        nbytes=1 << 20,
    )


def solution(mesh):
    fine = Mesh(mesh.devices.reshape(NZ, NYL, NX, NYH, NC), DP + TP)
    return jax.shard_map(
        local,
        mesh=fine,
        in_specs=(P(DP, TP), P(DP, None), P(DP), P(), P(DP, TP), P(TP)),
        out_specs=P(DP, TP),
        check_vma=False,
    )
```

```python
import jax
import jax.numpy as jnp
from jax import lax
from jax.experimental import pallas as pl
from jax.experimental.pallas import tpu as pltpu
from jax.sharding import Mesh
from jax.sharding import PartitionSpec as P

HEADS = 32
KV = 8
HEAD = 128
PER = HEADS // KV
EPSILON = 1e-06
ROPE_BASE = 1000000.0

NZ, NYL, NX, NYH, NC = 16, 2, 4, 4, 2
DP = ("z", "yl", "x")
TP = ("yh", "c")
WROWS = 32
ROWS = 256
HALF = 128
SAMPLES = 4
EXTRA = 16
NEAR = (1, 3, 0)
VMEM = 16 << 20


def call(kernel, out_shape, args, scalars=0, hbm=0, flops=0, nbytes=0, scratch=(), vmem_bytes=VMEM):
    smem = pl.BlockSpec(memory_space=pltpu.SMEM)
    vmem = pl.BlockSpec(memory_space=pltpu.VMEM)
    far = pl.BlockSpec(memory_space=pltpu.HBM)
    return pl.pallas_call(
        kernel,
        out_shape=out_shape,
        in_specs=[smem] * scalars + [far] * hbm + [vmem] * (len(args) - scalars - hbm),
        out_specs=[far] * len(out_shape) if isinstance(out_shape, list) else jax.tree.map(lambda _: vmem, out_shape),
        scratch_shapes=list(scratch),
        compiler_params=pltpu.CompilerParams(vmem_limit_bytes=vmem_bytes),
        cost_estimate=pl.CostEstimate(flops=flops, bytes_accessed=nbytes, transcendentals=0),
    )(*args)


def prepare_kernel(yl_ref, dp_ref, s_hbm, w_hbm, gain_ref, o_hbm, ow_hbm, s_ref, w_ref, o_ref, sems):
    load_s = pltpu.make_async_copy(s_hbm, s_ref, sems.at[0])
    load_w = pltpu.make_async_copy(w_hbm, w_ref, sems.at[1])
    load_s.start()
    load_w.start()
    yl, dp = yl_ref[0], dp_ref[0]
    lines = gain_ref.shape[0]
    line = lax.broadcasted_iota(jnp.int32, (lines, 128), 0)
    gain = jnp.where(line == lax.shift_right_logical(dp, 2), gain_ref[...].astype(jnp.float32), 0.0)
    gain = jnp.sum(gain, axis=0, keepdims=True)
    row = lax.broadcasted_iota(jnp.int32, (WROWS, 128), 0)
    lane = lax.broadcasted_iota(jnp.int32, (WROWS, 128), 1)
    gain = jnp.sum(jnp.where(lane == (dp & 3) * WROWS + row, gain, 0.0), axis=1, keepdims=True)
    source = lax.broadcasted_iota(jnp.int32, (512, 128), 0)
    r = lax.broadcasted_iota(jnp.int32, (512, 128), 1)
    rel, zz, k = lax.shift_right_logical(r, 6), lax.shift_right_logical(r, 5) & 1, r & 31
    base = zz * 256 + (rel ^ yl) * 128 + k
    load_s.wait()
    stores = []
    for x in range(NX):
        perm = (source == base + x * 32).astype(jnp.bfloat16)
        o_ref[x] = jnp.dot(s_ref[...], perm, preferred_element_type=jnp.float32).astype(jnp.bfloat16)
        for yh in range(NYH):
            copy = pltpu.make_async_copy(o_ref.at[x], o_hbm.at[yh, x], sems.at[3 + x * NYH + yh])
            copy.start()
            stores.append(copy)
    load_w.wait()
    w_ref[...] = (w_ref[...].astype(jnp.float32) * gain).astype(jnp.bfloat16)
    copy = pltpu.make_async_copy(w_ref, ow_hbm, sems.at[2])
    copy.start()
    stores.append(copy)
    for copy in stores:
        copy.wait()


def arrange_kernel(c_ref, wown_ref, woth_ref, w_ref):
    c = c_ref[0]
    for rel in range(NC):
        for yh in range(NYH):
            row = pl.multiple_of((yh * 4 + (c ^ rel) * 2) * WROWS, 64)
            at = (rel * NYH + yh) * 128
            w_ref[at : at + 64] = wown_ref[pl.ds(row, 64)]
            w_ref[at + 64 : at + 128] = woth_ref[pl.ds(row, 64)]


def first_kernel(x_at_ref, own_ref, oth_ref, w_ref, o_ref, x_ref):
    x = x_at_ref[0]

    def states(step):
        g = (x + step) & 3
        return jnp.concatenate([ref[g, yh] for ref in (own_ref, oth_ref) for yh in range(NYH)], axis=1)

    o_ref[...] = jnp.dot(states(2), w_ref[...], preferred_element_type=jnp.float32).astype(jnp.bfloat16)
    for n, step in enumerate(NEAR):
        x_ref[n] = states(step)


def second_kernel(x_ref, w_ref, o1_ref, o3_ref, own_ref):
    for n, ref in enumerate((o1_ref, o3_ref, own_ref)):
        ref[...] = jnp.dot(x_ref[n], w_ref[...], preferred_element_type=jnp.float32).astype(ref.dtype)


def tail_of(lens, moved):
    return sum(jnp.where(n >= SAMPLES - moved, lens[n], 0) for n in range(SAMPLES))


def attend_kernel(len_ref, moved_ref, p0_ref, p1_ref, p2_ref, sq_ref, sq2_ref, bias_ref, cos_ref, sin_ref, o_ref):
    s1 = len_ref[0]
    s2 = s1 + len_ref[1]
    s3 = s2 + len_ref[2]
    i = lax.broadcasted_iota(jnp.int32, (ROWS, ROWS), 0)
    j = lax.broadcasted_iota(jnp.int32, (ROWS, ROWS), 1)
    start = jnp.where(i >= s3, s3, jnp.where(i >= s2, s2, jnp.where(i >= s1, s1, 0)))
    allowed = ((j >= start) & (j <= i)).astype(jnp.int32)
    r = lax.rsqrt((sq_ref[...] + sq2_ref[...]) * (1.0 / (NZ * NYL * NX * WROWS)) + EPSILON)
    r = jnp.sum(jnp.where(i == j, r, 0.0), axis=1, keepdims=True)
    cos, sin = cos_ref[...], sin_ref[...]

    def head(n):
        at = n * HEAD
        total = p0_ref[:, at : at + HEAD]
        for ref in (p1_ref, p2_ref):
            total = total + ref[:, at : at + HEAD].astype(jnp.float32)
        return total * r + bias_ref[:, n * HEAD : (n + 1) * HEAD]

    def rotate(v):
        return (v * cos + pltpu.roll(v, HEAD // 2, 1) * sin).astype(jnp.bfloat16)

    key = rotate(head(PER))
    value = head(PER + 1).astype(jnp.bfloat16)
    for h in range(PER):
        query = rotate(head(h))
        for block in range(2):
            rows, keys = slice(block * HALF, (block + 1) * HALF), slice(0, (block + 1) * HALF)
            scores = lax.dot_general(
                query[rows], key[keys], (((1,), (1,)), ((), ())), preferred_element_type=jnp.float32
            )
            scores = jnp.where(allowed[rows, keys] > 0, scores * HEAD ** (-0.5), -1e30)
            e = jnp.exp(scores - jnp.max(scores, axis=1, keepdims=True))
            weights = (e * (1.0 / jnp.sum(e, axis=1, keepdims=True))).astype(jnp.bfloat16)
            o_ref[rows, h * HEAD : (h + 1) * HEAD] = jnp.dot(
                weights, value[keys], preferred_element_type=jnp.float32
            ).astype(jnp.bfloat16)
    tail = tail_of(len_ref, moved_ref[0]).astype(jnp.float32)
    o_ref[ROWS:] = jnp.full((EXTRA, PER * HEAD), tail, jnp.float32).astype(jnp.bfloat16)


def pack_kernel(len_ref, moved_ref, prev_ref, own_ref, o_hbm, o_ref, sems):
    tail = tail_of(len_ref, moved_ref[0])
    incoming = prev_ref[ROWS:, :HEAD].astype(jnp.float32)[:1, :1].astype(jnp.int32)
    row = lax.broadcasted_iota(jnp.int32, (ROWS, ROWS), 1)
    copies = []
    for block in range(2):
        slot = lax.broadcasted_iota(jnp.int32, (ROWS, ROWS), 0) + block * ROWS
        pick = ((row == slot - incoming) & (row < ROWS - tail)).astype(jnp.bfloat16)
        picked = jnp.dot(pick, own_ref[:ROWS], preferred_element_type=jnp.float32)
        if block == 0:
            pick = ((slot < incoming) & (row == slot + (ROWS - incoming))).astype(jnp.bfloat16)
            picked = picked + jnp.dot(pick, prev_ref[:ROWS], preferred_element_type=jnp.float32)
        o_ref[block] = picked.astype(jnp.bfloat16)
        copy = pltpu.make_async_copy(o_ref.at[block], o_hbm.at[pl.ds(block * ROWS, ROWS)], sems.at[block])
        copy.start()
        copies.append(copy)
    for copy in copies:
        copy.wait()


def local(states, lengths, moved, norm_gain, qkv_weight, qkv_bias):
    yl, c = lax.axis_index("yl"), lax.axis_index("c")
    dp = lax.axis_index(DP)
    bf = lambda *shape: jax.ShapeDtypeStruct(shape, jnp.bfloat16)

    columns = qkv_weight.shape[1]
    sent, scaled = call(
        prepare_kernel,
        [bf(NYH, NX, ROWS, 128), bf(WROWS, columns)],
        (yl.reshape(1), dp.reshape(1), states, qkv_weight, norm_gain.reshape(-1, 128)),
        2,
        2,
        flops=2 * 256 * 512 * 512,
        nbytes=1 << 20,
        scratch=[
            pltpu.VMEM((ROWS, 512), jnp.bfloat16),
            pltpu.VMEM((WROWS, columns), jnp.bfloat16),
            pltpu.VMEM((NX, ROWS, 128), jnp.bfloat16),
            pltpu.SemaphoreType.DMA((3 + NX * NYH,)),
        ],
        vmem_bytes=60 << 20,
    )
    raw = lax.all_to_all(sent, "yh", 0, 0, tiled=True)
    wown = lax.all_gather(scaled, "z", axis=0, tiled=True)
    raw, wown, lengths, moved, qkv_bias = lax.optimization_barrier((raw, wown, lengths, moved, qkv_bias))

    woth = lax.ppermute(wown, "yl", [(0, 1), (1, 0)])
    raw = lax.optimization_barrier(raw.transpose(1, 0, 2, 3))
    spread = lax.all_to_all(raw, "x", 0, 0, tiled=True)

    squares = jnp.sum(jnp.square(raw.astype(jnp.float32)), axis=(0, 1, 3))
    lens = lengths[0]
    ids = jnp.arange(ROWS, dtype=jnp.int32)
    starts = [jnp.sum(lens[:n]) for n in range(SAMPLES)]
    begin = jnp.zeros_like(ids)
    for n in range(1, SAMPLES):
        begin = jnp.where(ids >= starts[n], starts[n], begin)
    positions = (ids - begin).astype(jnp.float32)
    inv_freq = ROPE_BASE ** (-(2.0 * jnp.arange(HEAD // 2, dtype=jnp.float32)) / HEAD)
    angles = positions[:, None] * inv_freq[None, :]
    cos, sin = jnp.cos(angles), jnp.sin(angles)
    cos = jnp.concatenate([cos, cos], axis=1)
    sin = jnp.concatenate([-sin, sin], axis=1)
    bias = qkv_bias.astype(jnp.float32)[None, :]
    spread, squares, bias, cos, sin = lax.optimization_barrier((spread, squares, bias, cos, sin))
    other = lax.ppermute(spread, "c", [(0, 1), (1, 0)])

    x = lax.axis_index("x")
    whole = lambda step, v: lax.ppermute(v, "x", [(i, (i + step) % NX) for i in range(NX)])
    flops = 2 * ROWS * 1024 * columns
    weights = call(
        arrange_kernel, bf(1024, columns), (c.reshape(1), wown, woth), 1, flops=20 * 10**9, nbytes=3 << 20
    )
    far, near = call(
        first_kernel,
        (bf(ROWS, columns), bf(3, ROWS, 1024)),
        (x.reshape(1), spread, other, weights),
        1,
        flops=flops,
        nbytes=6 << 20,
    )
    far = whole(2, far)
    right, left, own = call(
        second_kernel,
        (bf(ROWS, columns), bf(ROWS, columns), jax.ShapeDtypeStruct((ROWS, columns), jnp.float32)),
        (near, weights),
        flops=3 * flops,
        nbytes=4 << 20,
    )
    right, left = whole(1, right), whole(3, left)
    own, squares = lax.optimization_barrier((own, squares))
    own = own + far.astype(jnp.float32)
    squares2 = lax.ppermute(squares, "c", [(0, 1), (1, 0)])
    context = call(
        attend_kernel,
        bf(ROWS + EXTRA, PER * HEAD),
        (lens, moved, own, right, left, squares.reshape(1, ROWS), squares2.reshape(1, ROWS), bias, cos, sin),
        2,
        flops=4 * 4 * ROWS * ROWS * HEAD,
        nbytes=3 << 20,
    )
    previous = lax.ppermute(context, DP, [(i, i + 1) for i in range(NZ * NYL * NX - 1)])
    return call(
        pack_kernel,
        [bf(2 * ROWS, PER * HEAD)],
        (lens, moved, previous, context),
        2,
        flops=4 * 512 * 256 * 512,
        nbytes=1 << 20,
        scratch=[pltpu.VMEM((2, ROWS, PER * HEAD), jnp.bfloat16), pltpu.SemaphoreType.DMA((2,))],
    )[0]


def solution(mesh):
    fine = Mesh(mesh.devices.reshape(NZ, NYL, NX, NYH, NC), DP + TP)
    return jax.shard_map(
        local,
        mesh=fine,
        in_specs=(P(DP, TP), P(DP, None), P(DP), P(), P(DP, TP), P(TP)),
        out_specs=P(DP, TP),
        check_vma=False,
    )
```

```python
import jax
import jax.numpy as jnp
from jax import lax
from jax.experimental import pallas as pl
from jax.experimental.pallas import tpu as pltpu
from jax.sharding import Mesh
from jax.sharding import PartitionSpec as P

HEADS = 32
KV = 8
HEAD = 128
PER = HEADS // KV
EPSILON = 1e-06
ROPE_BASE = 1000000.0

NZ, NYL, NX, NYH, NC = 16, 2, 4, 4, 2
DP = ("z", "yl", "x")
TP = ("yh", "c")
WROWS = 32
ROWS = 256
HALF = 128
SAMPLES = 4
EXTRA = 16
NEAR = (1, 3, 0)
VMEM = 16 << 20


def call(kernel, out_shape, args, scalars=0, hbm=0, flops=0, nbytes=0, scratch=(), vmem_bytes=VMEM):
    smem = pl.BlockSpec(memory_space=pltpu.SMEM)
    vmem = pl.BlockSpec(memory_space=pltpu.VMEM)
    far = pl.BlockSpec(memory_space=pltpu.HBM)
    return pl.pallas_call(
        kernel,
        out_shape=out_shape,
        in_specs=[smem] * scalars + [far] * hbm + [vmem] * (len(args) - scalars - hbm),
        out_specs=[far] * len(out_shape) if isinstance(out_shape, list) else jax.tree.map(lambda _: vmem, out_shape),
        scratch_shapes=list(scratch),
        compiler_params=pltpu.CompilerParams(vmem_limit_bytes=vmem_bytes),
        cost_estimate=pl.CostEstimate(flops=flops, bytes_accessed=nbytes, transcendentals=0),
    )(*args)


def prepare_kernel(yl_ref, dp_ref, s_hbm, w_hbm, gain_ref, o_hbm, ow_hbm, s_ref, w_ref, o_ref, sems):
    halves = [pl.ds(n * HALF, HALF) for n in range(2)]
    loads = [pltpu.make_async_copy(s_hbm.at[rows], s_ref.at[rows], sems.at[n]) for n, rows in enumerate(halves)]
    load_w = pltpu.make_async_copy(w_hbm, w_ref, sems.at[2])
    for copy in (loads[0], load_w, loads[1]):
        copy.start()
    yl, dp = yl_ref[0], dp_ref[0]
    line = lax.broadcasted_iota(jnp.int32, (gain_ref.shape[0], 128), 0)
    gain = jnp.where(line == lax.shift_right_logical(dp, 2), gain_ref[...].astype(jnp.float32), 0.0)
    gain = jnp.sum(gain, axis=0, keepdims=True)
    row = lax.broadcasted_iota(jnp.int32, (WROWS, 128), 0)
    lane = lax.broadcasted_iota(jnp.int32, (WROWS, 128), 1)
    gain = jnp.sum(jnp.where(lane == (dp & 3) * WROWS + row, gain, 0.0), axis=1, keepdims=True)
    source = lax.broadcasted_iota(jnp.int32, (512, 128), 0)
    r = lax.broadcasted_iota(jnp.int32, (512, 128), 1)
    rel, zz, k = lax.shift_right_logical(r, 6), lax.shift_right_logical(r, 5) & 1, r & 31
    base = zz * 256 + (rel ^ yl) * 128 + k
    perms = [(source == base + x * 32).astype(jnp.bfloat16) for x in range(NX)]
    stores = []
    for n, rows in enumerate(halves):
        loads[n].wait()
        for x in range(NX):
            o_ref[x, rows] = jnp.dot(s_ref[rows], perms[x], preferred_element_type=jnp.float32).astype(jnp.bfloat16)
        for yh in range(NYH):
            stores.append(pltpu.make_async_copy(o_ref.at[:, rows], o_hbm.at[yh, :, rows], sems.at[4 + n * NYH + yh]))
            stores[-1].start()
        if n == 0:
            load_w.wait()
            w_ref[...] = (w_ref[...].astype(jnp.float32) * gain).astype(jnp.bfloat16)
            stores.append(pltpu.make_async_copy(w_ref, ow_hbm, sems.at[3]))
            stores[-1].start()
    for copy in stores:
        copy.wait()


def arrange_kernel(c_ref, wown_ref, woth_ref, w_ref):
    c = c_ref[0]
    for rel in range(NC):
        for yh in range(NYH):
            row = pl.multiple_of((yh * 4 + (c ^ rel) * 2) * WROWS, 64)
            at = (rel * NYH + yh) * 128
            w_ref[at : at + 64] = wown_ref[pl.ds(row, 64)]
            w_ref[at + 64 : at + 128] = woth_ref[pl.ds(row, 64)]


def first_kernel(x_at_ref, own_ref, oth_ref, w_ref, o_ref, x_ref):
    x = x_at_ref[0]

    def states(step):
        g = (x + step) & 3
        return jnp.concatenate([ref[g, yh] for ref in (own_ref, oth_ref) for yh in range(NYH)], axis=1)

    o_ref[...] = jnp.dot(states(2), w_ref[...], preferred_element_type=jnp.float32).astype(jnp.bfloat16)
    for n, step in enumerate(NEAR):
        x_ref[n] = states(step)


def second_kernel(x_ref, w_ref, o1_ref, o3_ref, own_ref):
    for n, ref in enumerate((o1_ref, o3_ref, own_ref)):
        ref[...] = jnp.dot(x_ref[n], w_ref[...], preferred_element_type=jnp.float32).astype(ref.dtype)


def tail_of(lens, moved):
    return sum(jnp.where(n >= SAMPLES - moved, lens[n], 0) for n in range(SAMPLES))


def attend_kernel(len_ref, moved_ref, p0_ref, p1_ref, p2_ref, sq_ref, sq2_ref, bias_ref, cos_ref, sin_ref, o_ref):
    s1 = len_ref[0]
    s2 = s1 + len_ref[1]
    s3 = s2 + len_ref[2]
    i = lax.broadcasted_iota(jnp.int32, (ROWS, ROWS), 0)
    j = lax.broadcasted_iota(jnp.int32, (ROWS, ROWS), 1)
    start = jnp.where(i >= s3, s3, jnp.where(i >= s2, s2, jnp.where(i >= s1, s1, 0)))
    allowed = (j >= start) & (j <= i)
    r = lax.rsqrt((sq_ref[...] + sq2_ref[...]) * (1.0 / (NZ * NYL * NX * WROWS)) + EPSILON)
    r = jnp.sum(jnp.where(i == j, r, 0.0), axis=1, keepdims=True)
    cos, sin = cos_ref[...], sin_ref[...]

    def head(n):
        at = n * HEAD
        total = p0_ref[:, at : at + HEAD]
        for ref in (p1_ref, p2_ref):
            total = total + ref[:, at : at + HEAD].astype(jnp.float32)
        return total * r + bias_ref[:, n * HEAD : (n + 1) * HEAD]

    def rotate(v):
        return (v * cos + pltpu.roll(v, HEAD // 2, 1) * sin).astype(jnp.bfloat16)

    key = rotate(head(PER))
    value = head(PER + 1).astype(jnp.bfloat16)
    for h in range(PER):
        query = rotate(head(h))
        scores = lax.dot_general(query, key, (((1,), (1,)), ((), ())), preferred_element_type=jnp.float32)
        scores = jnp.where(allowed, scores * HEAD ** (-0.5), -1e30)
        e = jnp.exp(scores - jnp.max(scores, axis=1, keepdims=True))
        weights = (e * (1.0 / jnp.sum(e, axis=1, keepdims=True))).astype(jnp.bfloat16)
        o_ref[:ROWS, h * HEAD : (h + 1) * HEAD] = jnp.dot(
            weights, value, preferred_element_type=jnp.float32
        ).astype(jnp.bfloat16)
    tail = tail_of(len_ref, moved_ref[0]).astype(jnp.float32)
    o_ref[ROWS:] = jnp.full((EXTRA, PER * HEAD), tail, jnp.float32).astype(jnp.bfloat16)


def pack_kernel(len_ref, moved_ref, prev_ref, own_ref, o_hbm, o_ref, sems):
    tail = tail_of(len_ref, moved_ref[0])
    incoming = prev_ref[ROWS:, :HEAD].astype(jnp.float32)[:1, :1].astype(jnp.int32)
    row = lax.broadcasted_iota(jnp.int32, (ROWS, ROWS), 1)
    copies = []
    for block in range(2):
        slot = lax.broadcasted_iota(jnp.int32, (ROWS, ROWS), 0) + block * ROWS
        pick = ((row == slot - incoming) & (row < ROWS - tail)).astype(jnp.bfloat16)
        picked = jnp.dot(pick, own_ref[:ROWS], preferred_element_type=jnp.float32)
        if block == 0:
            pick = ((slot < incoming) & (row == slot + (ROWS - incoming))).astype(jnp.bfloat16)
            picked = picked + jnp.dot(pick, prev_ref[:ROWS], preferred_element_type=jnp.float32)
        o_ref[block] = picked.astype(jnp.bfloat16)
        copy = pltpu.make_async_copy(o_ref.at[block], o_hbm.at[pl.ds(block * ROWS, ROWS)], sems.at[block])
        copy.start()
        copies.append(copy)
    for copy in copies:
        copy.wait()


def local(states, lengths, moved, norm_gain, qkv_weight, qkv_bias):
    yl, c = lax.axis_index("yl"), lax.axis_index("c")
    dp = lax.axis_index(DP)
    bf = lambda *shape: jax.ShapeDtypeStruct(shape, jnp.bfloat16)

    columns = qkv_weight.shape[1]
    sent, scaled = call(
        prepare_kernel,
        [bf(NYH, NX, ROWS, 128), bf(WROWS, columns)],
        (yl.reshape(1), dp.reshape(1), states, qkv_weight, norm_gain.reshape(-1, 128)),
        2,
        2,
        flops=2 * 256 * 512 * 512,
        nbytes=1 << 20,
        scratch=[
            pltpu.VMEM((ROWS, 512), jnp.bfloat16),
            pltpu.VMEM((WROWS, columns), jnp.bfloat16),
            pltpu.VMEM((NX, ROWS, 128), jnp.bfloat16),
            pltpu.SemaphoreType.DMA((4 + 2 * NYH,)),
        ],
        vmem_bytes=60 << 20,
    )
    raw = lax.all_to_all(sent, "yh", 0, 0, tiled=True)
    wown = lax.all_gather(scaled, "z", axis=0, tiled=True)
    raw, wown, lengths, moved, qkv_bias = lax.optimization_barrier((raw, wown, lengths, moved, qkv_bias))

    woth = lax.ppermute(wown, "yl", [(0, 1), (1, 0)])
    raw = lax.optimization_barrier(raw.transpose(1, 0, 2, 3))
    spread = lax.all_to_all(raw, "x", 0, 0, tiled=True)

    squares = jnp.sum(jnp.square(raw.astype(jnp.float32)), axis=(0, 1, 3))
    lens = lengths[0]
    ids = jnp.arange(ROWS, dtype=jnp.int32)
    starts = [jnp.sum(lens[:n]) for n in range(SAMPLES)]
    begin = jnp.zeros_like(ids)
    for n in range(1, SAMPLES):
        begin = jnp.where(ids >= starts[n], starts[n], begin)
    positions = (ids - begin).astype(jnp.float32)
    inv_freq = ROPE_BASE ** (-(2.0 * jnp.arange(HEAD // 2, dtype=jnp.float32)) / HEAD)
    angles = positions[:, None] * inv_freq[None, :]
    cos, sin = jnp.cos(angles), jnp.sin(angles)
    cos = jnp.concatenate([cos, cos], axis=1)
    sin = jnp.concatenate([-sin, sin], axis=1)
    bias = qkv_bias.astype(jnp.float32)[None, :]
    spread, squares, bias, cos, sin = lax.optimization_barrier((spread, squares, bias, cos, sin))
    other = lax.ppermute(spread, "c", [(0, 1), (1, 0)])

    x = lax.axis_index("x")
    whole = lambda step, v: lax.ppermute(v, "x", [(i, (i + step) % NX) for i in range(NX)])
    flops = 2 * ROWS * 1024 * columns
    weights = call(
        arrange_kernel, bf(1024, columns), (c.reshape(1), wown, woth), 1, flops=20 * 10**9, nbytes=3 << 20
    )
    far, near = call(
        first_kernel,
        (bf(ROWS, columns), bf(3, ROWS, 1024)),
        (x.reshape(1), spread, other, weights),
        1,
        flops=flops,
        nbytes=6 << 20,
    )
    far = whole(2, far)
    right, left, own = call(
        second_kernel,
        (bf(ROWS, columns), bf(ROWS, columns), jax.ShapeDtypeStruct((ROWS, columns), jnp.float32)),
        (near, weights),
        flops=3 * flops,
        nbytes=4 << 20,
    )
    right, left = whole(1, right), whole(3, left)
    own, squares = lax.optimization_barrier((own, squares))
    own = own + far.astype(jnp.float32)
    squares2 = lax.ppermute(squares, "c", [(0, 1), (1, 0)])
    context = call(
        attend_kernel,
        bf(ROWS + EXTRA, PER * HEAD),
        (lens, moved, own, right, left, squares.reshape(1, ROWS), squares2.reshape(1, ROWS), bias, cos, sin),
        2,
        flops=4 * 4 * ROWS * ROWS * HEAD,
        nbytes=3 << 20,
    )
    previous = lax.ppermute(context, DP, [(i, i + 1) for i in range(NZ * NYL * NX - 1)])
    return call(
        pack_kernel,
        [bf(2 * ROWS, PER * HEAD)],
        (lens, moved, previous, context),
        2,
        flops=4 * 512 * 256 * 512,
        nbytes=1 << 20,
        scratch=[pltpu.VMEM((2, ROWS, PER * HEAD), jnp.bfloat16), pltpu.SemaphoreType.DMA((2,))],
    )[0]


def solution(mesh):
    fine = Mesh(mesh.devices.reshape(NZ, NYL, NX, NYH, NC), DP + TP)
    return jax.shard_map(
        local,
        mesh=fine,
        in_specs=(P(DP, TP), P(DP, None), P(DP), P(), P(DP, TP), P(TP)),
        out_specs=P(DP, TP),
        check_vma=False,
    )
```

```python
import jax
import jax.numpy as jnp
from jax import lax
from jax.experimental import pallas as pl
from jax.experimental.pallas import tpu as pltpu
from jax.sharding import Mesh
from jax.sharding import PartitionSpec as P

HEADS = 32
KV = 8
HEAD = 128
PER = HEADS // KV
EPSILON = 1e-06
ROPE_BASE = 1000000.0

NZ, NYL, NX, NYH, NC = 16, 2, 4, 4, 2
DP = ("z", "yl", "x")
TP = ("yh", "c")
WROWS = 32
ROWS = 256
HALF = 128
SAMPLES = 4
EXTRA = 16
NEAR = (1, 3, 0)
VMEM = 16 << 20


def call(kernel, out_shape, args, scalars=0, hbm=0, flops=0, nbytes=0, scratch=(), vmem_bytes=VMEM):
    smem = pl.BlockSpec(memory_space=pltpu.SMEM)
    vmem = pl.BlockSpec(memory_space=pltpu.VMEM)
    far = pl.BlockSpec(memory_space=pltpu.HBM)
    return pl.pallas_call(
        kernel,
        out_shape=out_shape,
        in_specs=[smem] * scalars + [far] * hbm + [vmem] * (len(args) - scalars - hbm),
        out_specs=[far] * len(out_shape) if isinstance(out_shape, list) else jax.tree.map(lambda _: vmem, out_shape),
        scratch_shapes=list(scratch),
        compiler_params=pltpu.CompilerParams(vmem_limit_bytes=vmem_bytes),
        cost_estimate=pl.CostEstimate(flops=flops, bytes_accessed=nbytes, transcendentals=0),
    )(*args)


def prepare_kernel(yl_ref, dp_ref, s_hbm, w_hbm, gain_ref, o_hbm, ow_hbm, s_ref, w_ref, o_ref, sems):
    halves = [pl.ds(n * HALF, HALF) for n in range(2)]
    loads = [pltpu.make_async_copy(s_hbm.at[rows], s_ref.at[rows], sems.at[n]) for n, rows in enumerate(halves)]
    load_w = pltpu.make_async_copy(w_hbm, w_ref, sems.at[2])
    for copy in (loads[0], load_w, loads[1]):
        copy.start()
    yl, dp = yl_ref[0], dp_ref[0]
    line = lax.broadcasted_iota(jnp.int32, (gain_ref.shape[0], 128), 0)
    gain = jnp.where(line == lax.shift_right_logical(dp, 2), gain_ref[...].astype(jnp.float32), 0.0)
    gain = jnp.sum(gain, axis=0, keepdims=True)
    row = lax.broadcasted_iota(jnp.int32, (WROWS, 128), 0)
    lane = lax.broadcasted_iota(jnp.int32, (WROWS, 128), 1)
    gain = jnp.sum(jnp.where(lane == (dp & 3) * WROWS + row, gain, 0.0), axis=1, keepdims=True)
    source = lax.broadcasted_iota(jnp.int32, (512, 256), 0)
    r = lax.broadcasted_iota(jnp.int32, (512, 256), 1)
    odd, rel, zz, k = [lax.shift_right_logical(r, n) & mask for n, mask in ((7, 1), (6, 1), (5, 1), (0, 31))]
    base = zz * 256 + (rel ^ yl) * 128 + odd * 32 + k
    perms = [(source == base + x * 32).astype(jnp.bfloat16) for x in range(0, NX, 2)]
    stores = []
    for n, rows in enumerate(halves):
        loads[n].wait()
        for x in range(0, NX, 2):
            pair = jnp.dot(s_ref[rows], perms[x // 2], preferred_element_type=jnp.float32).astype(jnp.bfloat16)
            o_ref[x, rows] = pair[:, :128]
            o_ref[x + 1, rows] = pair[:, 128:]
        for yh in range(NYH):
            stores.append(pltpu.make_async_copy(o_ref.at[:, rows], o_hbm.at[yh, :, rows], sems.at[4 + n * NYH + yh]))
            stores[-1].start()
        if n == 0:
            load_w.wait()
            w_ref[...] = (w_ref[...].astype(jnp.float32) * gain).astype(jnp.bfloat16)
            stores.append(pltpu.make_async_copy(w_ref, ow_hbm, sems.at[3]))
            stores[-1].start()
    for copy in stores:
        copy.wait()


def arrange_kernel(c_ref, wown_ref, woth_ref, w_ref):
    c = c_ref[0]
    for rel in range(NC):
        for yh in range(NYH):
            row = pl.multiple_of((yh * 4 + (c ^ rel) * 2) * WROWS, 64)
            at = (rel * NYH + yh) * 128
            w_ref[at : at + 64] = wown_ref[pl.ds(row, 64)]
            w_ref[at + 64 : at + 128] = woth_ref[pl.ds(row, 64)]


def first_kernel(x_at_ref, own_ref, oth_ref, w_ref, o_ref, x_ref):
    x = x_at_ref[0]

    def states(step):
        g = (x + step) & 3
        return jnp.concatenate([ref[g, yh] for ref in (own_ref, oth_ref) for yh in range(NYH)], axis=1)

    o_ref[...] = jnp.dot(states(2), w_ref[...], preferred_element_type=jnp.float32).astype(jnp.bfloat16)
    for n, step in enumerate(NEAR):
        x_ref[n] = states(step)


def second_kernel(x_ref, w_ref, o1_ref, o3_ref):
    for n, ref in enumerate((o1_ref, o3_ref)):
        ref[...] = jnp.dot(x_ref[n], w_ref[...], preferred_element_type=jnp.float32).astype(ref.dtype)


def own_kernel(x_ref, w_ref, o_ref):
    o_ref[...] = jnp.dot(x_ref[2], w_ref[...], preferred_element_type=jnp.float32)


def tail_of(lens, moved):
    return sum(jnp.where(n >= SAMPLES - moved, lens[n], 0) for n in range(SAMPLES))


def attend_kernel(len_ref, moved_ref, p0_ref, p1_ref, p2_ref, sq_ref, sq2_ref, bias_ref, cos_ref, sin_ref, o_ref, sent_ref):
    s1 = len_ref[0]
    s2 = s1 + len_ref[1]
    s3 = s2 + len_ref[2]
    i = lax.broadcasted_iota(jnp.int32, (ROWS, ROWS), 0)
    j = lax.broadcasted_iota(jnp.int32, (ROWS, ROWS), 1)
    start = jnp.where(i >= s3, s3, jnp.where(i >= s2, s2, jnp.where(i >= s1, s1, 0)))
    allowed = (j >= start) & (j <= i)
    r = lax.rsqrt((sq_ref[...] + sq2_ref[...]) * (1.0 / (NZ * NYL * NX * WROWS)) + EPSILON)
    r = jnp.sum(jnp.where(i == j, r, 0.0), axis=1, keepdims=True)
    cos, sin = cos_ref[...], sin_ref[...]

    def head(n):
        at = n * HEAD
        total = p0_ref[:, at : at + HEAD]
        for ref in (p1_ref, p2_ref):
            total = total + ref[:, at : at + HEAD].astype(jnp.float32)
        return total * r + bias_ref[:, n * HEAD : (n + 1) * HEAD]

    def rotate(v):
        return (v * cos + pltpu.roll(v, HEAD // 2, 1) * sin).astype(jnp.bfloat16)

    key = rotate(head(PER))
    value = head(PER + 1).astype(jnp.bfloat16)
    for h in range(PER):
        query = rotate(head(h))
        scores = lax.dot_general(query, key, (((1,), (1,)), ((), ())), preferred_element_type=jnp.float32)
        scores = jnp.where(allowed, scores * HEAD ** (-0.5), -1e30)
        e = jnp.exp(scores - jnp.max(scores, axis=1, keepdims=True))
        weights = (e * (1.0 / jnp.sum(e, axis=1, keepdims=True))).astype(jnp.bfloat16)
        o_ref[:, h * HEAD : (h + 1) * HEAD] = jnp.dot(
            weights, value, preferred_element_type=jnp.float32
        ).astype(jnp.bfloat16)
    tail = tail_of(len_ref, moved_ref[0]).astype(jnp.float32)
    sent_ref[EXTRA:] = o_ref[EXTRA:]
    top = o_ref[:EXTRA].astype(jnp.float32)
    row = lax.broadcasted_iota(jnp.int32, top.shape, 0)
    sent_ref[:EXTRA] = jnp.where(row == 0, tail, top).astype(jnp.bfloat16)


def pack_kernel(len_ref, moved_ref, prev_ref, own_ref, o_hbm, o_ref, sems):
    tail = tail_of(len_ref, moved_ref[0])
    incoming = prev_ref[:EXTRA, :HEAD].astype(jnp.float32)[:1, :1].astype(jnp.int32)
    row = lax.broadcasted_iota(jnp.int32, (ROWS, ROWS), 1)
    copies = []
    for block in range(2):
        slot = lax.broadcasted_iota(jnp.int32, (ROWS, ROWS), 0) + block * ROWS
        pick = ((row == slot - incoming) & (row < ROWS - tail)).astype(jnp.bfloat16)
        picked = jnp.dot(pick, own_ref[...], preferred_element_type=jnp.float32)
        if block == 0:
            pick = ((slot < incoming) & (row == slot + (ROWS - incoming))).astype(jnp.bfloat16)
            picked = picked + jnp.dot(pick, prev_ref[...], preferred_element_type=jnp.float32)
        o_ref[block] = picked.astype(jnp.bfloat16)
        copy = pltpu.make_async_copy(o_ref.at[block], o_hbm.at[pl.ds(block * ROWS, ROWS)], sems.at[block])
        copy.start()
        copies.append(copy)
    for copy in copies:
        copy.wait()


def local(states, lengths, moved, norm_gain, qkv_weight, qkv_bias):
    yl, c = lax.axis_index("yl"), lax.axis_index("c")
    dp = lax.axis_index(DP)
    bf = lambda *shape: jax.ShapeDtypeStruct(shape, jnp.bfloat16)

    columns = qkv_weight.shape[1]
    sent, scaled = call(
        prepare_kernel,
        [bf(NYH, NX, ROWS, 128), bf(WROWS, columns)],
        (yl.reshape(1), dp.reshape(1), states, qkv_weight, norm_gain.reshape(-1, 128)),
        2,
        2,
        flops=2 * 256 * 512 * 512,
        nbytes=1 << 20,
        scratch=[
            pltpu.VMEM((ROWS, 512), jnp.bfloat16),
            pltpu.VMEM((WROWS, columns), jnp.bfloat16),
            pltpu.VMEM((NX, ROWS, 128), jnp.bfloat16),
            pltpu.SemaphoreType.DMA((4 + 2 * NYH,)),
        ],
        vmem_bytes=60 << 20,
    )
    raw = lax.all_to_all(sent, "yh", 0, 0, tiled=True)
    wown = lax.all_gather(scaled, "z", axis=0, tiled=True)
    raw, wown, lengths, moved, qkv_bias = lax.optimization_barrier((raw, wown, lengths, moved, qkv_bias))

    woth = lax.ppermute(wown, "yl", [(0, 1), (1, 0)])
    raw = lax.optimization_barrier(raw.transpose(1, 0, 2, 3))
    spread = lax.all_to_all(raw, "x", 0, 0, tiled=True)

    squares = jnp.sum(jnp.square(raw.astype(jnp.float32)), axis=(0, 1, 3))
    lens = lengths[0]
    ids = jnp.arange(ROWS, dtype=jnp.int32)
    starts = [jnp.sum(lens[:n]) for n in range(SAMPLES)]
    begin = jnp.zeros_like(ids)
    for n in range(1, SAMPLES):
        begin = jnp.where(ids >= starts[n], starts[n], begin)
    positions = (ids - begin).astype(jnp.float32)
    inv_freq = ROPE_BASE ** (-(2.0 * jnp.arange(HEAD // 2, dtype=jnp.float32)) / HEAD)
    angles = positions[:, None] * inv_freq[None, :]
    cos, sin = jnp.cos(angles), jnp.sin(angles)
    cos = jnp.concatenate([cos, cos], axis=1)
    sin = jnp.concatenate([-sin, sin], axis=1)
    bias = qkv_bias.astype(jnp.float32)[None, :]
    spread, squares, bias, cos, sin = lax.optimization_barrier((spread, squares, bias, cos, sin))
    other = lax.ppermute(spread, "c", [(0, 1), (1, 0)])

    x = lax.axis_index("x")
    whole = lambda step, v: lax.ppermute(v, "x", [(i, (i + step) % NX) for i in range(NX)])
    flops = 2 * ROWS * 1024 * columns
    weights = call(
        arrange_kernel, bf(1024, columns), (c.reshape(1), wown, woth), 1, flops=20 * 10**9, nbytes=3 << 20
    )
    far, near = call(
        first_kernel,
        (bf(ROWS, columns), bf(3, ROWS, 1024)),
        (x.reshape(1), spread, other, weights),
        1,
        flops=flops,
        nbytes=6 << 20,
    )
    far = whole(2, far)
    right, left = call(
        second_kernel,
        (bf(ROWS, columns), bf(ROWS, columns)),
        (near, weights),
        flops=2 * flops,
        nbytes=4 << 20,
    )
    own = call(
        own_kernel, jax.ShapeDtypeStruct((ROWS, columns), jnp.float32), (near, weights), flops=flops, nbytes=3 << 20
    )
    right, left = whole(1, right), whole(3, left)
    own, squares = lax.optimization_barrier((own, squares))
    own = own + far.astype(jnp.float32)
    squares2 = lax.ppermute(squares, "c", [(0, 1), (1, 0)])
    context, sent = call(
        attend_kernel,
        (bf(ROWS, PER * HEAD), bf(ROWS, PER * HEAD)),
        (lens, moved, own, right, left, squares.reshape(1, ROWS), squares2.reshape(1, ROWS), bias, cos, sin),
        2,
        flops=4 * 4 * ROWS * ROWS * HEAD,
        nbytes=3 << 20,
    )
    previous = lax.ppermute(sent, DP, [(i, i + 1) for i in range(NZ * NYL * NX - 1)])
    return call(
        pack_kernel,
        [bf(2 * ROWS, PER * HEAD)],
        (lens, moved, previous, context),
        2,
        flops=4 * 512 * 256 * 512,
        nbytes=1 << 20,
        scratch=[pltpu.VMEM((2, ROWS, PER * HEAD), jnp.bfloat16), pltpu.SemaphoreType.DMA((2,))],
    )[0]


def solution(mesh):
    fine = Mesh(mesh.devices.reshape(NZ, NYL, NX, NYH, NC), DP + TP)
    return jax.shard_map(
        local,
        mesh=fine,
        in_specs=(P(DP, TP), P(DP, None), P(DP), P(), P(DP, TP), P(TP)),
        out_specs=P(DP, TP),
        check_vma=False,
    )
```

```python
import jax
import jax.numpy as jnp
from jax import lax
from jax.experimental import pallas as pl
from jax.experimental.pallas import tpu as pltpu
from jax.sharding import Mesh
from jax.sharding import PartitionSpec as P

HEADS = 32
KV = 8
HEAD = 128
PER = HEADS // KV
EPSILON = 1e-06
ROPE_BASE = 1000000.0

NZ, NYL, NX, NYH, NC = 16, 2, 4, 4, 2
DP = ("z", "yl", "x")
TP = ("yh", "c")
WROWS = 32
ROWS = 256
HALF = 128
SAMPLES = 4
EXTRA = 16
VMEM = 16 << 20


def call(kernel, out_shape, args, scalars=0, hbm=0, flops=0, nbytes=0, scratch=(), vmem_bytes=VMEM):
    smem = pl.BlockSpec(memory_space=pltpu.SMEM)
    vmem = pl.BlockSpec(memory_space=pltpu.VMEM)
    far = pl.BlockSpec(memory_space=pltpu.HBM)
    return pl.pallas_call(
        kernel,
        out_shape=out_shape,
        in_specs=[smem] * scalars + [far] * hbm + [vmem] * (len(args) - scalars - hbm),
        out_specs=[far] * len(out_shape) if isinstance(out_shape, list) else jax.tree.map(lambda _: vmem, out_shape),
        scratch_shapes=list(scratch),
        compiler_params=pltpu.CompilerParams(vmem_limit_bytes=vmem_bytes),
        cost_estimate=pl.CostEstimate(flops=flops, bytes_accessed=nbytes, transcendentals=0),
    )(*args)


def prepare_kernel(yl_ref, dp_ref, s_hbm, w_hbm, gain_ref, o_hbm, ow_hbm, s_ref, w_ref, o_ref, sems):
    halves = [pl.ds(n * HALF, HALF) for n in range(2)]
    loads = [pltpu.make_async_copy(s_hbm.at[rows], s_ref.at[rows], sems.at[n]) for n, rows in enumerate(halves)]
    load_w = pltpu.make_async_copy(w_hbm, w_ref, sems.at[2])
    for copy in (loads[0], load_w, loads[1]):
        copy.start()
    yl, dp = yl_ref[0], dp_ref[0]
    line = lax.broadcasted_iota(jnp.int32, (gain_ref.shape[0], 128), 0)
    gain = jnp.where(line == lax.shift_right_logical(dp, 2), gain_ref[...].astype(jnp.float32), 0.0)
    gain = jnp.sum(gain, axis=0, keepdims=True)
    row = lax.broadcasted_iota(jnp.int32, (WROWS, 128), 0)
    lane = lax.broadcasted_iota(jnp.int32, (WROWS, 128), 1)
    gain = jnp.sum(jnp.where(lane == (dp & 3) * WROWS + row, gain, 0.0), axis=1, keepdims=True)
    source = lax.broadcasted_iota(jnp.int32, (512, 256), 0)
    r = lax.broadcasted_iota(jnp.int32, (512, 256), 1)
    odd, rel, zz, k = [lax.shift_right_logical(r, n) & mask for n, mask in ((7, 1), (6, 1), (5, 1), (0, 31))]
    base = zz * 256 + (rel ^ yl) * 128 + odd * 32 + k
    perms = [(source == base + x * 32).astype(jnp.bfloat16) for x in range(0, NX, 2)]
    stores = []
    for n, rows in enumerate(halves):
        loads[n].wait()
        for x in range(0, NX, 2):
            pair = jnp.dot(s_ref[rows], perms[x // 2], preferred_element_type=jnp.float32).astype(jnp.bfloat16)
            o_ref[x, rows] = pair[:, :128]
            o_ref[x + 1, rows] = pair[:, 128:]
        for yh in range(NYH):
            stores.append(pltpu.make_async_copy(o_ref.at[:, rows], o_hbm.at[yh, :, rows], sems.at[4 + n * NYH + yh]))
            stores[-1].start()
        if n == 0:
            load_w.wait()
            w_ref[...] = (w_ref[...].astype(jnp.float32) * gain).astype(jnp.bfloat16)
            stores.append(pltpu.make_async_copy(w_ref, ow_hbm, sems.at[3]))
            stores[-1].start()
    for copy in stores:
        copy.wait()


def arrange_kernel(c_ref, wown_ref, woth_ref, w_ref):
    c = c_ref[0]
    for rel in range(NC):
        for yh in range(NYH):
            row = pl.multiple_of((yh * 4 + (c ^ rel) * 2) * WROWS, 64)
            at = (rel * NYH + yh) * 128
            w_ref[at : at + 64] = wown_ref[pl.ds(row, 64)]
            w_ref[at + 64 : at + 128] = woth_ref[pl.ds(row, 64)]


def product_kernel(own_ref, oth_ref, w_ref, o_hbm, o_ref, sems):
    copies = []
    for g in range(NX):
        x = jnp.concatenate([ref[g, yh] for ref in (own_ref, oth_ref) for yh in range(NYH)], axis=1)
        o_ref[g] = jnp.dot(x, w_ref[...], preferred_element_type=jnp.float32).astype(jnp.bfloat16)
        copies.append(pltpu.make_async_copy(o_ref.at[g], o_hbm.at[g], sems.at[g]))
        copies[-1].start()
    for copy in copies:
        copy.wait()


def tail_of(lens, moved):
    return sum(jnp.where(n >= SAMPLES - moved, lens[n], 0) for n in range(SAMPLES))


def attend_kernel(len_ref, moved_ref, p_ref, sq_ref, sq2_ref, bias_ref, cos_ref, sin_ref, o_ref, sent_ref):
    s1 = len_ref[0]
    s2 = s1 + len_ref[1]
    s3 = s2 + len_ref[2]
    i = lax.broadcasted_iota(jnp.int32, (ROWS, ROWS), 0)
    j = lax.broadcasted_iota(jnp.int32, (ROWS, ROWS), 1)
    start = jnp.where(i >= s3, s3, jnp.where(i >= s2, s2, jnp.where(i >= s1, s1, 0)))
    allowed = (j >= start) & (j <= i)
    r = lax.rsqrt((sq_ref[...] + sq2_ref[...]) * (1.0 / (NZ * NYL * NX * WROWS)) + EPSILON)
    r = jnp.sum(jnp.where(i == j, r, 0.0), axis=1, keepdims=True)
    cos, sin = cos_ref[...], sin_ref[...]

    def head(n):
        at = n * HEAD
        total = p_ref[0, :, at : at + HEAD].astype(jnp.float32)
        for k in range(1, NX):
            total = total + p_ref[k, :, at : at + HEAD].astype(jnp.float32)
        return total * r + bias_ref[:, n * HEAD : (n + 1) * HEAD]

    def rotate(v):
        return (v * cos + pltpu.roll(v, HEAD // 2, 1) * sin).astype(jnp.bfloat16)

    key = rotate(head(PER))
    value = head(PER + 1).astype(jnp.bfloat16)
    for h in range(PER):
        query = rotate(head(h))
        scores = lax.dot_general(query, key, (((1,), (1,)), ((), ())), preferred_element_type=jnp.float32)
        scores = jnp.where(allowed, scores * HEAD ** (-0.5), -1e30)
        e = jnp.exp(scores - jnp.max(scores, axis=1, keepdims=True))
        weights = (e * (1.0 / jnp.sum(e, axis=1, keepdims=True))).astype(jnp.bfloat16)
        o_ref[:, h * HEAD : (h + 1) * HEAD] = jnp.dot(
            weights, value, preferred_element_type=jnp.float32
        ).astype(jnp.bfloat16)
    tail = tail_of(len_ref, moved_ref[0]).astype(jnp.float32)
    sent_ref[EXTRA:] = o_ref[EXTRA:]
    top = o_ref[:EXTRA].astype(jnp.float32)
    row = lax.broadcasted_iota(jnp.int32, top.shape, 0)
    sent_ref[:EXTRA] = jnp.where(row == 0, tail, top).astype(jnp.bfloat16)


def pack_kernel(len_ref, moved_ref, prev_ref, own_ref, o_hbm, o_ref, sems):
    tail = tail_of(len_ref, moved_ref[0])
    incoming = prev_ref[:EXTRA, :HEAD].astype(jnp.float32)[:1, :1].astype(jnp.int32)
    row = lax.broadcasted_iota(jnp.int32, (ROWS, ROWS), 1)
    copies = []
    for block in range(2):
        slot = lax.broadcasted_iota(jnp.int32, (ROWS, ROWS), 0) + block * ROWS
        pick = ((row == slot - incoming) & (row < ROWS - tail)).astype(jnp.bfloat16)
        picked = jnp.dot(pick, own_ref[...], preferred_element_type=jnp.float32)
        if block == 0:
            pick = ((slot < incoming) & (row == slot + (ROWS - incoming))).astype(jnp.bfloat16)
            picked = picked + jnp.dot(pick, prev_ref[...], preferred_element_type=jnp.float32)
        o_ref[block] = picked.astype(jnp.bfloat16)
        copy = pltpu.make_async_copy(o_ref.at[block], o_hbm.at[pl.ds(block * ROWS, ROWS)], sems.at[block])
        copy.start()
        copies.append(copy)
    for copy in copies:
        copy.wait()


def local(states, lengths, moved, norm_gain, qkv_weight, qkv_bias):
    yl, c = lax.axis_index("yl"), lax.axis_index("c")
    dp = lax.axis_index(DP)
    bf = lambda *shape: jax.ShapeDtypeStruct(shape, jnp.bfloat16)

    columns = qkv_weight.shape[1]
    sent, scaled = call(
        prepare_kernel,
        [bf(NYH, NX, ROWS, 128), bf(WROWS, columns)],
        (yl.reshape(1), dp.reshape(1), states, qkv_weight, norm_gain.reshape(-1, 128)),
        2,
        2,
        flops=2 * 256 * 512 * 512,
        nbytes=1 << 20,
        scratch=[
            pltpu.VMEM((ROWS, 512), jnp.bfloat16),
            pltpu.VMEM((WROWS, columns), jnp.bfloat16),
            pltpu.VMEM((NX, ROWS, 128), jnp.bfloat16),
            pltpu.SemaphoreType.DMA((4 + 2 * NYH,)),
        ],
        vmem_bytes=60 << 20,
    )
    raw = lax.all_to_all(sent, "yh", 0, 0, tiled=True)
    wown = lax.all_gather(scaled, "z", axis=0, tiled=True)
    raw, wown, lengths, moved, qkv_bias = lax.optimization_barrier((raw, wown, lengths, moved, qkv_bias))

    woth = lax.ppermute(wown, "yl", [(0, 1), (1, 0)])
    raw = lax.optimization_barrier(raw.transpose(1, 0, 2, 3))
    spread = lax.all_to_all(raw, "x", 0, 0, tiled=True)

    squares = jnp.sum(jnp.square(raw.astype(jnp.float32)), axis=(0, 1, 3))
    lens = lengths[0]
    ids = jnp.arange(ROWS, dtype=jnp.int32)
    starts = [jnp.sum(lens[:n]) for n in range(SAMPLES)]
    begin = jnp.zeros_like(ids)
    for n in range(1, SAMPLES):
        begin = jnp.where(ids >= starts[n], starts[n], begin)
    positions = (ids - begin).astype(jnp.float32)
    inv_freq = ROPE_BASE ** (-(2.0 * jnp.arange(HEAD // 2, dtype=jnp.float32)) / HEAD)
    angles = positions[:, None] * inv_freq[None, :]
    cos, sin = jnp.cos(angles), jnp.sin(angles)
    cos = jnp.concatenate([cos, cos], axis=1)
    sin = jnp.concatenate([-sin, sin], axis=1)
    bias = qkv_bias.astype(jnp.float32)[None, :]
    spread, squares, bias, cos, sin = lax.optimization_barrier((spread, squares, bias, cos, sin))
    other = lax.ppermute(spread, "c", [(0, 1), (1, 0)])

    weights = call(
        arrange_kernel, bf(1024, columns), (c.reshape(1), wown, woth), 1, flops=20 * 10**9, nbytes=3 << 20
    )
    partial = call(
        product_kernel,
        [bf(NX, ROWS, columns)],
        (spread, other, weights),
        flops=2 * NX * ROWS * 1024 * columns,
        nbytes=6 << 20,
        scratch=[pltpu.VMEM((NX, ROWS, columns), jnp.bfloat16), pltpu.SemaphoreType.DMA((NX,))],
    )[0]
    partial, squares = lax.optimization_barrier((partial, squares))
    summed = lax.all_to_all(partial, "x", 0, 0, tiled=True)
    squares2 = lax.ppermute(squares, "c", [(0, 1), (1, 0)])
    context, sent = call(
        attend_kernel,
        (bf(ROWS, PER * HEAD), bf(ROWS, PER * HEAD)),
        (lens, moved, summed, squares.reshape(1, ROWS), squares2.reshape(1, ROWS), bias, cos, sin),
        2,
        flops=4 * 4 * ROWS * ROWS * HEAD,
        nbytes=3 << 20,
    )
    previous = lax.ppermute(sent, DP, [(i, i + 1) for i in range(NZ * NYL * NX - 1)])
    return call(
        pack_kernel,
        [bf(2 * ROWS, PER * HEAD)],
        (lens, moved, previous, context),
        2,
        flops=4 * 512 * 256 * 512,
        nbytes=1 << 20,
        scratch=[pltpu.VMEM((2, ROWS, PER * HEAD), jnp.bfloat16), pltpu.SemaphoreType.DMA((2,))],
    )[0]


def solution(mesh):
    fine = Mesh(mesh.devices.reshape(NZ, NYL, NX, NYH, NC), DP + TP)
    return jax.shard_map(
        local,
        mesh=fine,
        in_specs=(P(DP, TP), P(DP, None), P(DP), P(), P(DP, TP), P(TP)),
        out_specs=P(DP, TP),
        check_vma=False,
    )
```

```python
import jax
import jax.numpy as jnp
from jax import lax
from jax.experimental import pallas as pl
from jax.experimental.pallas import tpu as pltpu
from jax.sharding import Mesh
from jax.sharding import PartitionSpec as P

HEADS = 32
KV = 8
HEAD = 128
PER = HEADS // KV
EPSILON = 1e-06
ROPE_BASE = 1000000.0

NZ, NYL, NX, NYH, NC = 16, 2, 4, 4, 2
DP = ("z", "yl", "x")
TP = ("yh", "c")
WROWS = 32
ROWS = 256
HALF = 128
SAMPLES = 4
EXTRA = 16
VMEM = 16 << 20


def call(kernel, out_shape, args, scalars=0, hbm=0, flops=0, nbytes=0, scratch=(), vmem_bytes=VMEM):
    smem = pl.BlockSpec(memory_space=pltpu.SMEM)
    vmem = pl.BlockSpec(memory_space=pltpu.VMEM)
    far = pl.BlockSpec(memory_space=pltpu.HBM)
    return pl.pallas_call(
        kernel,
        out_shape=out_shape,
        in_specs=[smem] * scalars + [far] * hbm + [vmem] * (len(args) - scalars - hbm),
        out_specs=[far] * len(out_shape) if isinstance(out_shape, list) else jax.tree.map(lambda _: vmem, out_shape),
        scratch_shapes=list(scratch),
        compiler_params=pltpu.CompilerParams(vmem_limit_bytes=vmem_bytes),
        cost_estimate=pl.CostEstimate(flops=flops, bytes_accessed=nbytes, transcendentals=0),
    )(*args)


def prepare_kernel(yl_ref, dp_ref, s_hbm, w_hbm, gain_ref, o_hbm, ow_hbm, s_ref, w_ref, o_ref, sems):
    halves = [pl.ds(n * HALF, HALF) for n in range(2)]
    loads = [pltpu.make_async_copy(s_hbm.at[rows], s_ref.at[rows], sems.at[n]) for n, rows in enumerate(halves)]
    load_w = pltpu.make_async_copy(w_hbm, w_ref, sems.at[2])
    for copy in (loads[0], load_w, loads[1]):
        copy.start()
    yl, dp = yl_ref[0], dp_ref[0]
    line = lax.broadcasted_iota(jnp.int32, (gain_ref.shape[0], 128), 0)
    gain = jnp.where(line == lax.shift_right_logical(dp, 2), gain_ref[...].astype(jnp.float32), 0.0)
    gain = jnp.sum(gain, axis=0, keepdims=True)
    row = lax.broadcasted_iota(jnp.int32, (WROWS, 128), 0)
    lane = lax.broadcasted_iota(jnp.int32, (WROWS, 128), 1)
    gain = jnp.sum(jnp.where(lane == (dp & 3) * WROWS + row, gain, 0.0), axis=1, keepdims=True)
    source = lax.broadcasted_iota(jnp.int32, (512, 256), 0)
    r = lax.broadcasted_iota(jnp.int32, (512, 256), 1)
    odd, rel, zz, k = [lax.shift_right_logical(r, n) & mask for n, mask in ((7, 1), (6, 1), (5, 1), (0, 31))]
    base = zz * 256 + (rel ^ yl) * 128 + odd * 32 + k
    perms = [(source == base + x * 32).astype(jnp.bfloat16) for x in range(0, NX, 2)]
    stores = []
    for n, rows in enumerate(halves):
        loads[n].wait()
        for x in range(0, NX, 2):
            pair = jnp.dot(s_ref[rows], perms[x // 2], preferred_element_type=jnp.float32).astype(jnp.bfloat16)
            o_ref[x, rows] = pair[:, :128]
            o_ref[x + 1, rows] = pair[:, 128:]
        for yh in range(NYH):
            stores.append(pltpu.make_async_copy(o_ref.at[:, rows], o_hbm.at[yh, :, rows], sems.at[4 + n * NYH + yh]))
            stores[-1].start()
        if n == 0:
            load_w.wait()
            w_ref[...] = (w_ref[...].astype(jnp.float32) * gain).astype(jnp.bfloat16)
            stores.append(pltpu.make_async_copy(w_ref, ow_hbm, sems.at[3]))
            stores[-1].start()
    for copy in stores:
        copy.wait()


def arrange_kernel(c_ref, wown_ref, woth_ref, w_ref):
    c = c_ref[0]
    for rel in range(NC):
        for yh in range(NYH):
            row = pl.multiple_of((yh * 4 + (c ^ rel) * 2) * WROWS, 64)
            at = (rel * NYH + yh) * 128
            w_ref[at : at + 64] = wown_ref[pl.ds(row, 64)]
            w_ref[at + 64 : at + 128] = woth_ref[pl.ds(row, 64)]


def product_kernel(x_at_ref, own_ref, oth_ref, w_ref, o2_ref, o1_ref, o3_ref, x_ref):
    for step, o_ref in ((2, o2_ref), (1, o1_ref), (3, o3_ref), (0, x_ref)):
        g = (x_at_ref[0] + step) & 3
        x = jnp.concatenate([ref[g, yh] for ref in (own_ref, oth_ref) for yh in range(NYH)], axis=1)
        if step == 0:
            o_ref[...] = x
        else:
            o_ref[...] = jnp.dot(x, w_ref[...], preferred_element_type=jnp.float32).astype(jnp.bfloat16)


def own_kernel(x_ref, w_ref, o_ref):
    o_ref[...] = jnp.dot(x_ref[...], w_ref[...], preferred_element_type=jnp.float32)


def tail_of(lens, moved):
    return sum(jnp.where(n >= SAMPLES - moved, lens[n], 0) for n in range(SAMPLES))


def attend_kernel(len_ref, moved_ref, p0_ref, p1_ref, p2_ref, sq_ref, sq2_ref, bias_ref, cos_ref, sin_ref, o_ref, sent_ref):
    s1 = len_ref[0]
    s2 = s1 + len_ref[1]
    s3 = s2 + len_ref[2]
    i = lax.broadcasted_iota(jnp.int32, (ROWS, ROWS), 0)
    j = lax.broadcasted_iota(jnp.int32, (ROWS, ROWS), 1)
    start = jnp.where(i >= s3, s3, jnp.where(i >= s2, s2, jnp.where(i >= s1, s1, 0)))
    allowed = (j >= start) & (j <= i)
    r = lax.rsqrt((sq_ref[...] + sq2_ref[...]) * (1.0 / (NZ * NYL * NX * WROWS)) + EPSILON)
    r = jnp.sum(jnp.where(i == j, r, 0.0), axis=1, keepdims=True)
    cos, sin = cos_ref[...], sin_ref[...]

    def head(n):
        at = n * HEAD
        total = p0_ref[:, at : at + HEAD]
        for ref in (p1_ref, p2_ref):
            total = total + ref[:, at : at + HEAD].astype(jnp.float32)
        return total * r + bias_ref[:, n * HEAD : (n + 1) * HEAD]

    def rotate(v):
        return (v * cos + pltpu.roll(v, HEAD // 2, 1) * sin).astype(jnp.bfloat16)

    key = rotate(head(PER))
    value = head(PER + 1).astype(jnp.bfloat16)
    for h in range(PER):
        query = rotate(head(h))
        scores = lax.dot_general(query, key, (((1,), (1,)), ((), ())), preferred_element_type=jnp.float32)
        scores = jnp.where(allowed, scores * HEAD ** (-0.5), -1e30)
        e = jnp.exp(scores - jnp.max(scores, axis=1, keepdims=True))
        weights = (e * (1.0 / jnp.sum(e, axis=1, keepdims=True))).astype(jnp.bfloat16)
        o_ref[:, h * HEAD : (h + 1) * HEAD] = jnp.dot(
            weights, value, preferred_element_type=jnp.float32
        ).astype(jnp.bfloat16)
    tail = tail_of(len_ref, moved_ref[0]).astype(jnp.float32)
    sent_ref[EXTRA:] = o_ref[EXTRA:]
    top = o_ref[:EXTRA].astype(jnp.float32)
    row = lax.broadcasted_iota(jnp.int32, top.shape, 0)
    sent_ref[:EXTRA] = jnp.where(row == 0, tail, top).astype(jnp.bfloat16)


def pack_kernel(len_ref, moved_ref, prev_ref, own_ref, o_hbm, o_ref, sems):
    tail = tail_of(len_ref, moved_ref[0])
    incoming = prev_ref[:EXTRA, :HEAD].astype(jnp.float32)[:1, :1].astype(jnp.int32)
    row = lax.broadcasted_iota(jnp.int32, (ROWS, ROWS), 1)
    copies = []
    for block in range(2):
        slot = lax.broadcasted_iota(jnp.int32, (ROWS, ROWS), 0) + block * ROWS
        pick = ((row == slot - incoming) & (row < ROWS - tail)).astype(jnp.bfloat16)
        picked = jnp.dot(pick, own_ref[...], preferred_element_type=jnp.float32)
        if block == 0:
            pick = ((slot < incoming) & (row == slot + (ROWS - incoming))).astype(jnp.bfloat16)
            picked = picked + jnp.dot(pick, prev_ref[...], preferred_element_type=jnp.float32)
        o_ref[block] = picked.astype(jnp.bfloat16)
        copy = pltpu.make_async_copy(o_ref.at[block], o_hbm.at[pl.ds(block * ROWS, ROWS)], sems.at[block])
        copy.start()
        copies.append(copy)
    for copy in copies:
        copy.wait()


def local(states, lengths, moved, norm_gain, qkv_weight, qkv_bias):
    yl, c = lax.axis_index("yl"), lax.axis_index("c")
    dp = lax.axis_index(DP)
    bf = lambda *shape: jax.ShapeDtypeStruct(shape, jnp.bfloat16)

    columns = qkv_weight.shape[1]
    sent, scaled = call(
        prepare_kernel,
        [bf(NYH, NX, ROWS, 128), bf(WROWS, columns)],
        (yl.reshape(1), dp.reshape(1), states, qkv_weight, norm_gain.reshape(-1, 128)),
        2,
        2,
        flops=2 * 256 * 512 * 512,
        nbytes=1 << 20,
        scratch=[
            pltpu.VMEM((ROWS, 512), jnp.bfloat16),
            pltpu.VMEM((WROWS, columns), jnp.bfloat16),
            pltpu.VMEM((NX, ROWS, 128), jnp.bfloat16),
            pltpu.SemaphoreType.DMA((4 + 2 * NYH,)),
        ],
        vmem_bytes=60 << 20,
    )
    raw = lax.all_to_all(sent, "yh", 0, 0, tiled=True)
    wown = lax.all_gather(scaled, "z", axis=0, tiled=True)
    raw, wown, lengths, moved, qkv_bias = lax.optimization_barrier((raw, wown, lengths, moved, qkv_bias))

    woth = lax.ppermute(wown, "yl", [(0, 1), (1, 0)])
    raw = lax.optimization_barrier(raw.transpose(1, 0, 2, 3))
    spread = lax.all_to_all(raw, "x", 0, 0, tiled=True)

    squares = jnp.sum(jnp.square(raw.astype(jnp.float32)), axis=(0, 1, 3))
    lens = lengths[0]
    ids = jnp.arange(ROWS, dtype=jnp.int32)
    starts = [jnp.sum(lens[:n]) for n in range(SAMPLES)]
    begin = jnp.zeros_like(ids)
    for n in range(1, SAMPLES):
        begin = jnp.where(ids >= starts[n], starts[n], begin)
    positions = (ids - begin).astype(jnp.float32)
    inv_freq = ROPE_BASE ** (-(2.0 * jnp.arange(HEAD // 2, dtype=jnp.float32)) / HEAD)
    angles = positions[:, None] * inv_freq[None, :]
    cos, sin = jnp.cos(angles), jnp.sin(angles)
    cos = jnp.concatenate([cos, cos], axis=1)
    sin = jnp.concatenate([-sin, sin], axis=1)
    bias = qkv_bias.astype(jnp.float32)[None, :]
    spread, squares, bias, cos, sin = lax.optimization_barrier((spread, squares, bias, cos, sin))
    other = lax.ppermute(spread, "c", [(0, 1), (1, 0)])

    x = lax.axis_index("x")
    whole = lambda step, v: lax.ppermute(v, "x", [(i, (i + step) % NX) for i in range(NX)])
    flops = 2 * ROWS * 1024 * columns
    weights = call(
        arrange_kernel, bf(1024, columns), (c.reshape(1), wown, woth), 1, flops=20 * 10**9, nbytes=3 << 20
    )
    far, right, left, near = call(
        product_kernel,
        (bf(ROWS, columns),) * 3 + (bf(ROWS, 1024),),
        (x.reshape(1), spread, other, weights),
        1,
        flops=3 * flops,
        nbytes=6 << 20,
    )
    far = whole(2, far)
    own = call(
        own_kernel, jax.ShapeDtypeStruct((ROWS, columns), jnp.float32), (near, weights), flops=flops, nbytes=3 << 20
    )
    right, left = whole(1, right), whole(3, left)
    own, squares = lax.optimization_barrier((own, squares))
    own = own + far.astype(jnp.float32)
    squares2 = lax.ppermute(squares, "c", [(0, 1), (1, 0)])
    context, sent = call(
        attend_kernel,
        (bf(ROWS, PER * HEAD), bf(ROWS, PER * HEAD)),
        (lens, moved, own, right, left, squares.reshape(1, ROWS), squares2.reshape(1, ROWS), bias, cos, sin),
        2,
        flops=4 * 4 * ROWS * ROWS * HEAD,
        nbytes=3 << 20,
    )
    previous = lax.ppermute(sent, DP, [(i, i + 1) for i in range(NZ * NYL * NX - 1)])
    return call(
        pack_kernel,
        [bf(2 * ROWS, PER * HEAD)],
        (lens, moved, previous, context),
        2,
        flops=4 * 512 * 256 * 512,
        nbytes=1 << 20,
        scratch=[pltpu.VMEM((2, ROWS, PER * HEAD), jnp.bfloat16), pltpu.SemaphoreType.DMA((2,))],
    )[0]


def solution(mesh):
    fine = Mesh(mesh.devices.reshape(NZ, NYL, NX, NYH, NC), DP + TP)
    return jax.shard_map(
        local,
        mesh=fine,
        in_specs=(P(DP, TP), P(DP, None), P(DP), P(), P(DP, TP), P(TP)),
        out_specs=P(DP, TP),
        check_vma=False,
    )
```

```python
import jax
import jax.numpy as jnp
from jax import lax
from jax.experimental import pallas as pl
from jax.experimental.pallas import tpu as pltpu
from jax.sharding import Mesh
from jax.sharding import PartitionSpec as P

HEADS = 32
KV = 8
HEAD = 128
PER = HEADS // KV
EPSILON = 1e-06
ROPE_BASE = 1000000.0

NZ, NYL, NX, NYH, NC = 16, 2, 4, 4, 2
DP = ("z", "yl", "x")
TP = ("yh", "c")
WROWS = 32
ROWS = 256
HALF = 128
SAMPLES = 4
EXTRA = 16
NEAR = (3, 2, 0)
VMEM = 16 << 20


def call(kernel, out_shape, args, scalars=0, hbm=0, flops=0, nbytes=0, scratch=(), vmem_bytes=VMEM):
    smem = pl.BlockSpec(memory_space=pltpu.SMEM)
    vmem = pl.BlockSpec(memory_space=pltpu.VMEM)
    far = pl.BlockSpec(memory_space=pltpu.HBM)
    return pl.pallas_call(
        kernel,
        out_shape=out_shape,
        in_specs=[smem] * scalars + [far] * hbm + [vmem] * (len(args) - scalars - hbm),
        out_specs=[far] * len(out_shape) if isinstance(out_shape, list) else jax.tree.map(lambda _: vmem, out_shape),
        scratch_shapes=list(scratch),
        compiler_params=pltpu.CompilerParams(vmem_limit_bytes=vmem_bytes),
        cost_estimate=pl.CostEstimate(flops=flops, bytes_accessed=nbytes, transcendentals=0),
    )(*args)


def prepare_kernel(yl_ref, dp_ref, s_hbm, w_hbm, gain_ref, o_hbm, ow_hbm, s_ref, w_ref, o_ref, sems):
    halves = [pl.ds(n * HALF, HALF) for n in range(2)]
    loads = [pltpu.make_async_copy(s_hbm.at[rows], s_ref.at[rows], sems.at[n]) for n, rows in enumerate(halves)]
    load_w = pltpu.make_async_copy(w_hbm, w_ref, sems.at[2])
    for copy in (loads[0], load_w, loads[1]):
        copy.start()
    yl, dp = yl_ref[0], dp_ref[0]
    line = lax.broadcasted_iota(jnp.int32, (gain_ref.shape[0], 128), 0)
    gain = jnp.where(line == lax.shift_right_logical(dp, 2), gain_ref[...].astype(jnp.float32), 0.0)
    gain = jnp.sum(gain, axis=0, keepdims=True)
    row = lax.broadcasted_iota(jnp.int32, (WROWS, 128), 0)
    lane = lax.broadcasted_iota(jnp.int32, (WROWS, 128), 1)
    gain = jnp.sum(jnp.where(lane == (dp & 3) * WROWS + row, gain, 0.0), axis=1, keepdims=True)
    source = lax.broadcasted_iota(jnp.int32, (512, 256), 0)
    r = lax.broadcasted_iota(jnp.int32, (512, 256), 1)
    odd, rel, zz, k = [lax.shift_right_logical(r, n) & mask for n, mask in ((7, 1), (6, 1), (5, 1), (0, 31))]
    base = zz * 256 + (rel ^ yl) * 128 + odd * 32 + k
    perms = [(source == base + x * 32).astype(jnp.bfloat16) for x in range(0, NX, 2)]
    stores = []
    for n, rows in enumerate(halves):
        loads[n].wait()
        for x in range(0, NX, 2):
            pair = jnp.dot(s_ref[rows], perms[x // 2], preferred_element_type=jnp.float32).astype(jnp.bfloat16)
            o_ref[x, rows] = pair[:, :128]
            o_ref[x + 1, rows] = pair[:, 128:]
        for yh in range(NYH):
            stores.append(pltpu.make_async_copy(o_ref.at[:, rows], o_hbm.at[yh, :, rows], sems.at[4 + n * NYH + yh]))
            stores[-1].start()
        if n == 0:
            load_w.wait()
            w_ref[...] = (w_ref[...].astype(jnp.float32) * gain).astype(jnp.bfloat16)
            stores.append(pltpu.make_async_copy(w_ref, ow_hbm, sems.at[3]))
            stores[-1].start()
    for copy in stores:
        copy.wait()


def arrange_kernel(c_ref, wown_ref, woth_ref, w_ref):
    c = c_ref[0]
    for rel in range(NC):
        for yh in range(NYH):
            row = pl.multiple_of((yh * 4 + (c ^ rel) * 2) * WROWS, 64)
            at = (rel * NYH + yh) * 128
            w_ref[at : at + 64] = wown_ref[pl.ds(row, 64)]
            w_ref[at + 64 : at + 128] = woth_ref[pl.ds(row, 64)]


def first_kernel(x_at_ref, own_ref, oth_ref, w_ref, o_ref, x_ref):
    x = x_at_ref[0]

    def states(step):
        g = (x + step) & 3
        return jnp.concatenate([ref[g, yh] for ref in (own_ref, oth_ref) for yh in range(NYH)], axis=1)

    o_ref[...] = jnp.dot(states(1), w_ref[...], preferred_element_type=jnp.float32).astype(jnp.bfloat16)
    for n, step in enumerate(NEAR):
        x_ref[n] = states(step)


def second_kernel(x_ref, w_ref, o1_ref, o3_ref):
    for n, ref in enumerate((o1_ref, o3_ref)):
        ref[...] = jnp.dot(x_ref[n], w_ref[...], preferred_element_type=jnp.float32).astype(ref.dtype)


def own_kernel(x_ref, w_ref, o_ref):
    o_ref[...] = jnp.dot(x_ref[2], w_ref[...], preferred_element_type=jnp.float32)


def tail_of(lens, moved):
    return sum(jnp.where(n >= SAMPLES - moved, lens[n], 0) for n in range(SAMPLES))


def attend_kernel(len_ref, moved_ref, p0_ref, p1_ref, p2_ref, sq_ref, sq2_ref, bias_ref, cos_ref, sin_ref, o_ref, sent_ref):
    s1 = len_ref[0]
    s2 = s1 + len_ref[1]
    s3 = s2 + len_ref[2]
    i = lax.broadcasted_iota(jnp.int32, (ROWS, ROWS), 0)
    j = lax.broadcasted_iota(jnp.int32, (ROWS, ROWS), 1)
    start = jnp.where(i >= s3, s3, jnp.where(i >= s2, s2, jnp.where(i >= s1, s1, 0)))
    allowed = (j >= start) & (j <= i)
    r = lax.rsqrt((sq_ref[...] + sq2_ref[...]) * (1.0 / (NZ * NYL * NX * WROWS)) + EPSILON)
    r = jnp.sum(jnp.where(i == j, r, 0.0), axis=1, keepdims=True)
    cos, sin = cos_ref[...], sin_ref[...]

    def head(n):
        at = n * HEAD
        total = p0_ref[:, at : at + HEAD]
        for ref in (p1_ref, p2_ref):
            total = total + ref[:, at : at + HEAD].astype(jnp.float32)
        return total * r + bias_ref[:, n * HEAD : (n + 1) * HEAD]

    def rotate(v):
        return (v * cos + pltpu.roll(v, HEAD // 2, 1) * sin).astype(jnp.bfloat16)

    key = rotate(head(PER))
    value = head(PER + 1).astype(jnp.bfloat16)
    for h in range(PER):
        query = rotate(head(h))
        scores = lax.dot_general(query, key, (((1,), (1,)), ((), ())), preferred_element_type=jnp.float32)
        scores = jnp.where(allowed, scores * HEAD ** (-0.5), -1e30)
        e = jnp.exp(scores - jnp.max(scores, axis=1, keepdims=True))
        weights = (e * (1.0 / jnp.sum(e, axis=1, keepdims=True))).astype(jnp.bfloat16)
        o_ref[:, h * HEAD : (h + 1) * HEAD] = jnp.dot(
            weights, value, preferred_element_type=jnp.float32
        ).astype(jnp.bfloat16)
    tail = tail_of(len_ref, moved_ref[0]).astype(jnp.float32)
    sent_ref[EXTRA:] = o_ref[EXTRA:]
    top = o_ref[:EXTRA].astype(jnp.float32)
    row = lax.broadcasted_iota(jnp.int32, top.shape, 0)
    sent_ref[:EXTRA] = jnp.where(row == 0, tail, top).astype(jnp.bfloat16)


def pack_kernel(len_ref, moved_ref, prev_ref, own_ref, o_hbm, o_ref, sems):
    tail = tail_of(len_ref, moved_ref[0])
    incoming = prev_ref[:EXTRA, :HEAD].astype(jnp.float32)[:1, :1].astype(jnp.int32)
    row = lax.broadcasted_iota(jnp.int32, (ROWS, ROWS), 1)
    copies = []
    for block in range(2):
        slot = lax.broadcasted_iota(jnp.int32, (ROWS, ROWS), 0) + block * ROWS
        pick = ((row == slot - incoming) & (row < ROWS - tail)).astype(jnp.bfloat16)
        picked = jnp.dot(pick, own_ref[...], preferred_element_type=jnp.float32)
        if block == 0:
            pick = ((slot < incoming) & (row == slot + (ROWS - incoming))).astype(jnp.bfloat16)
            picked = picked + jnp.dot(pick, prev_ref[...], preferred_element_type=jnp.float32)
        o_ref[block] = picked.astype(jnp.bfloat16)
        copy = pltpu.make_async_copy(o_ref.at[block], o_hbm.at[pl.ds(block * ROWS, ROWS)], sems.at[block])
        copy.start()
        copies.append(copy)
    for copy in copies:
        copy.wait()


def local(states, lengths, moved, norm_gain, qkv_weight, qkv_bias):
    yl, c = lax.axis_index("yl"), lax.axis_index("c")
    dp = lax.axis_index(DP)
    bf = lambda *shape: jax.ShapeDtypeStruct(shape, jnp.bfloat16)

    columns = qkv_weight.shape[1]
    sent, scaled = call(
        prepare_kernel,
        [bf(NYH, NX, ROWS, 128), bf(WROWS, columns)],
        (yl.reshape(1), dp.reshape(1), states, qkv_weight, norm_gain.reshape(-1, 128)),
        2,
        2,
        flops=2 * 256 * 512 * 512,
        nbytes=1 << 20,
        scratch=[
            pltpu.VMEM((ROWS, 512), jnp.bfloat16),
            pltpu.VMEM((WROWS, columns), jnp.bfloat16),
            pltpu.VMEM((NX, ROWS, 128), jnp.bfloat16),
            pltpu.SemaphoreType.DMA((4 + 2 * NYH,)),
        ],
        vmem_bytes=60 << 20,
    )
    raw = lax.all_to_all(sent, "yh", 0, 0, tiled=True)
    wown = lax.all_gather(scaled, "z", axis=0, tiled=True)
    raw, wown, lengths, moved, qkv_bias = lax.optimization_barrier((raw, wown, lengths, moved, qkv_bias))

    woth = lax.ppermute(wown, "yl", [(0, 1), (1, 0)])
    raw = lax.optimization_barrier(raw.transpose(1, 0, 2, 3))
    spread = lax.all_to_all(raw, "x", 0, 0, tiled=True)

    squares = jnp.sum(jnp.square(raw.astype(jnp.float32)), axis=(0, 1, 3))
    lens = lengths[0]
    ids = jnp.arange(ROWS, dtype=jnp.int32)
    starts = [jnp.sum(lens[:n]) for n in range(SAMPLES)]
    begin = jnp.zeros_like(ids)
    for n in range(1, SAMPLES):
        begin = jnp.where(ids >= starts[n], starts[n], begin)
    positions = (ids - begin).astype(jnp.float32)
    inv_freq = ROPE_BASE ** (-(2.0 * jnp.arange(HEAD // 2, dtype=jnp.float32)) / HEAD)
    angles = positions[:, None] * inv_freq[None, :]
    cos, sin = jnp.cos(angles), jnp.sin(angles)
    cos = jnp.concatenate([cos, cos], axis=1)
    sin = jnp.concatenate([-sin, sin], axis=1)
    bias = qkv_bias.astype(jnp.float32)[None, :]
    spread, squares, bias, cos, sin = lax.optimization_barrier((spread, squares, bias, cos, sin))
    other = lax.ppermute(spread, "c", [(0, 1), (1, 0)])

    x = lax.axis_index("x")
    whole = lambda step, v: lax.ppermute(v, "x", [(i, (i + step) % NX) for i in range(NX)])
    flops = 2 * ROWS * 1024 * columns
    weights = call(
        arrange_kernel, bf(1024, columns), (c.reshape(1), wown, woth), 1, flops=20 * 10**9, nbytes=3 << 20
    )
    right, near = call(
        first_kernel,
        (bf(ROWS, columns), bf(3, ROWS, 1024)),
        (x.reshape(1), spread, other, weights),
        1,
        flops=flops,
        nbytes=6 << 20,
    )
    right = whole(1, right)
    left, far = call(
        second_kernel,
        (bf(ROWS, columns), bf(ROWS, columns)),
        (near, weights),
        flops=2 * flops,
        nbytes=4 << 20,
    )
    own = call(
        own_kernel, jax.ShapeDtypeStruct((ROWS, columns), jnp.float32), (near, weights), flops=flops, nbytes=3 << 20
    )
    left, far = whole(3, left), whole(2, far)
    own, squares = lax.optimization_barrier((own, squares))
    own = own + right.astype(jnp.float32)
    squares2 = lax.ppermute(squares, "c", [(0, 1), (1, 0)])
    context, sent = call(
        attend_kernel,
        (bf(ROWS, PER * HEAD), bf(ROWS, PER * HEAD)),
        (lens, moved, own, left, far, squares.reshape(1, ROWS), squares2.reshape(1, ROWS), bias, cos, sin),
        2,
        flops=4 * 4 * ROWS * ROWS * HEAD,
        nbytes=3 << 20,
    )
    previous = lax.ppermute(sent, DP, [(i, i + 1) for i in range(NZ * NYL * NX - 1)])
    return call(
        pack_kernel,
        [bf(2 * ROWS, PER * HEAD)],
        (lens, moved, previous, context),
        2,
        flops=4 * 512 * 256 * 512,
        nbytes=1 << 20,
        scratch=[pltpu.VMEM((2, ROWS, PER * HEAD), jnp.bfloat16), pltpu.SemaphoreType.DMA((2,))],
    )[0]


def solution(mesh):
    fine = Mesh(mesh.devices.reshape(NZ, NYL, NX, NYH, NC), DP + TP)
    return jax.shard_map(
        local,
        mesh=fine,
        in_specs=(P(DP, TP), P(DP, None), P(DP), P(), P(DP, TP), P(TP)),
        out_specs=P(DP, TP),
        check_vma=False,
    )
```

```python
import functools

import jax
import jax.numpy as jnp
from jax import lax
from jax.experimental import pallas as pl
from jax.experimental.pallas import tpu as pltpu
from jax.sharding import Mesh
from jax.sharding import PartitionSpec as P

HEADS = 32
KV = 8
HEAD = 128
PER = HEADS // KV
EPSILON = 1e-06
ROPE_BASE = 1000000.0

NZ, NYL, NX, NYH, NC = 16, 2, 4, 4, 2
DP = ("z", "yl", "x")
TP = ("yh", "c")
WROWS = 32
ROWS = 256
HALF = 128
SAMPLES = 4
EXTRA = 16
VMEM = 16 << 20


def call(kernel, out_shape, args, scalars=0, hbm=0, flops=0, nbytes=0, scratch=(), vmem_bytes=VMEM):
    smem = pl.BlockSpec(memory_space=pltpu.SMEM)
    vmem = pl.BlockSpec(memory_space=pltpu.VMEM)
    far = pl.BlockSpec(memory_space=pltpu.HBM)
    return pl.pallas_call(
        kernel,
        out_shape=out_shape,
        in_specs=[smem] * scalars + [far] * hbm + [vmem] * (len(args) - scalars - hbm),
        out_specs=[far] * len(out_shape) if isinstance(out_shape, list) else jax.tree.map(lambda _: vmem, out_shape),
        scratch_shapes=list(scratch),
        compiler_params=pltpu.CompilerParams(vmem_limit_bytes=vmem_bytes),
        cost_estimate=pl.CostEstimate(flops=flops, bytes_accessed=nbytes, transcendentals=0),
    )(*args)


def prepare_kernel(yl_ref, dp_ref, s_hbm, w_hbm, gain_ref, o_hbm, ow_hbm, s_ref, w_ref, o_ref, sems):
    halves = [pl.ds(n * HALF, HALF) for n in range(2)]
    loads = [pltpu.make_async_copy(s_hbm.at[rows], s_ref.at[rows], sems.at[n]) for n, rows in enumerate(halves)]
    load_w = pltpu.make_async_copy(w_hbm, w_ref, sems.at[2])
    for copy in (loads[0], load_w, loads[1]):
        copy.start()
    yl, dp = yl_ref[0], dp_ref[0]
    line = lax.broadcasted_iota(jnp.int32, (gain_ref.shape[0], 128), 0)
    gain = jnp.where(line == lax.shift_right_logical(dp, 2), gain_ref[...].astype(jnp.float32), 0.0)
    gain = jnp.sum(gain, axis=0, keepdims=True)
    row = lax.broadcasted_iota(jnp.int32, (WROWS, 128), 0)
    lane = lax.broadcasted_iota(jnp.int32, (WROWS, 128), 1)
    gain = jnp.sum(jnp.where(lane == (dp & 3) * WROWS + row, gain, 0.0), axis=1, keepdims=True)
    source = lax.broadcasted_iota(jnp.int32, (512, 256), 0)
    r = lax.broadcasted_iota(jnp.int32, (512, 256), 1)
    odd, rel, zz, k = [lax.shift_right_logical(r, n) & mask for n, mask in ((7, 1), (6, 1), (5, 1), (0, 31))]
    base = zz * 256 + (rel ^ yl) * 128 + odd * 32 + k
    perms = [(source == base + x * 32).astype(jnp.bfloat16) for x in range(0, NX, 2)]
    stores = []
    for n, rows in enumerate(halves):
        loads[n].wait()
        for x in range(0, NX, 2):
            pair = jnp.dot(s_ref[rows], perms[x // 2], preferred_element_type=jnp.float32).astype(jnp.bfloat16)
            o_ref[x, rows] = pair[:, :128]
            o_ref[x + 1, rows] = pair[:, 128:]
        for yh in range(NYH):
            stores.append(pltpu.make_async_copy(o_ref.at[:, rows], o_hbm.at[yh, :, rows], sems.at[4 + n * NYH + yh]))
            stores[-1].start()
        if n == 0:
            load_w.wait()
            w_ref[...] = (w_ref[...].astype(jnp.float32) * gain).astype(jnp.bfloat16)
            stores.append(pltpu.make_async_copy(w_ref, ow_hbm, sems.at[3]))
            stores[-1].start()
    for copy in stores:
        copy.wait()


def arrange_kernel(c_ref, wown_ref, woth_ref, w_ref):
    c = c_ref[0]
    for rel in range(NC):
        for yh in range(NYH):
            row = pl.multiple_of((yh * 4 + (c ^ rel) * 2) * WROWS, 64)
            at = (rel * NYH + yh) * 128
            w_ref[at : at + 64] = wown_ref[pl.ds(row, 64)]
            w_ref[at + 64 : at + 128] = woth_ref[pl.ds(row, 64)]


def product_kernel(steps, x_at_ref, own_ref, oth_ref, w_ref, *o_refs):
    for step, o_ref in zip(steps, o_refs):
        g = (x_at_ref[0] + step) & 3
        x = jnp.concatenate([ref[g, yh] for ref in (own_ref, oth_ref) for yh in range(NYH)], axis=1)
        o_ref[...] = jnp.dot(x, w_ref[...], preferred_element_type=jnp.float32).astype(o_ref.dtype)


def tail_of(lens, moved):
    return sum(jnp.where(n >= SAMPLES - moved, lens[n], 0) for n in range(SAMPLES))


def attend_kernel(len_ref, moved_ref, p0_ref, p1_ref, p2_ref, sq_ref, sq2_ref, bias_ref, cos_ref, sin_ref, o_ref, sent_ref):
    s1 = len_ref[0]
    s2 = s1 + len_ref[1]
    s3 = s2 + len_ref[2]
    i = lax.broadcasted_iota(jnp.int32, (ROWS, ROWS), 0)
    j = lax.broadcasted_iota(jnp.int32, (ROWS, ROWS), 1)
    start = jnp.where(i >= s3, s3, jnp.where(i >= s2, s2, jnp.where(i >= s1, s1, 0)))
    allowed = (j >= start) & (j <= i)
    r = lax.rsqrt((sq_ref[...] + sq2_ref[...]) * (1.0 / (NZ * NYL * NX * WROWS)) + EPSILON)
    r = jnp.sum(jnp.where(i == j, r, 0.0), axis=1, keepdims=True)
    cos, sin = cos_ref[...], sin_ref[...]

    def head(n):
        at = n * HEAD
        total = p0_ref[:, at : at + HEAD]
        for ref in (p1_ref, p2_ref):
            total = total + ref[:, at : at + HEAD].astype(jnp.float32)
        return total * r + bias_ref[:, n * HEAD : (n + 1) * HEAD]

    def rotate(v):
        return (v * cos + pltpu.roll(v, HEAD // 2, 1) * sin).astype(jnp.bfloat16)

    key = rotate(head(PER))
    value = head(PER + 1).astype(jnp.bfloat16)
    for h in range(PER):
        query = rotate(head(h))
        scores = lax.dot_general(query, key, (((1,), (1,)), ((), ())), preferred_element_type=jnp.float32)
        scores = jnp.where(allowed, scores * HEAD ** (-0.5), -1e30)
        e = jnp.exp(scores - jnp.max(scores, axis=1, keepdims=True))
        weights = (e * (1.0 / jnp.sum(e, axis=1, keepdims=True))).astype(jnp.bfloat16)
        o_ref[:, h * HEAD : (h + 1) * HEAD] = jnp.dot(
            weights, value, preferred_element_type=jnp.float32
        ).astype(jnp.bfloat16)
    tail = tail_of(len_ref, moved_ref[0]).astype(jnp.float32)
    sent_ref[EXTRA:] = o_ref[EXTRA:]
    top = o_ref[:EXTRA].astype(jnp.float32)
    row = lax.broadcasted_iota(jnp.int32, top.shape, 0)
    sent_ref[:EXTRA] = jnp.where(row == 0, tail, top).astype(jnp.bfloat16)


def pack_kernel(len_ref, moved_ref, prev_ref, own_ref, o_hbm, o_ref, sems):
    tail = tail_of(len_ref, moved_ref[0])
    incoming = prev_ref[:EXTRA, :HEAD].astype(jnp.float32)[:1, :1].astype(jnp.int32)
    row = lax.broadcasted_iota(jnp.int32, (ROWS, ROWS), 1)
    copies = []
    for block in range(2):
        slot = lax.broadcasted_iota(jnp.int32, (ROWS, ROWS), 0) + block * ROWS
        pick = ((row == slot - incoming) & (row < ROWS - tail)).astype(jnp.bfloat16)
        picked = jnp.dot(pick, own_ref[...], preferred_element_type=jnp.float32)
        if block == 0:
            pick = ((slot < incoming) & (row == slot + (ROWS - incoming))).astype(jnp.bfloat16)
            picked = picked + jnp.dot(pick, prev_ref[...], preferred_element_type=jnp.float32)
        o_ref[block] = picked.astype(jnp.bfloat16)
        copy = pltpu.make_async_copy(o_ref.at[block], o_hbm.at[pl.ds(block * ROWS, ROWS)], sems.at[block])
        copy.start()
        copies.append(copy)
    for copy in copies:
        copy.wait()


def local(states, lengths, moved, norm_gain, qkv_weight, qkv_bias):
    yl, c = lax.axis_index("yl"), lax.axis_index("c")
    dp = lax.axis_index(DP)
    bf = lambda *shape: jax.ShapeDtypeStruct(shape, jnp.bfloat16)

    columns = qkv_weight.shape[1]
    sent, scaled = call(
        prepare_kernel,
        [bf(NYH, NX, ROWS, 128), bf(WROWS, columns)],
        (yl.reshape(1), dp.reshape(1), states, qkv_weight, norm_gain.reshape(-1, 128)),
        2,
        2,
        flops=2 * 256 * 512 * 512,
        nbytes=1 << 20,
        scratch=[
            pltpu.VMEM((ROWS, 512), jnp.bfloat16),
            pltpu.VMEM((WROWS, columns), jnp.bfloat16),
            pltpu.VMEM((NX, ROWS, 128), jnp.bfloat16),
            pltpu.SemaphoreType.DMA((4 + 2 * NYH,)),
        ],
        vmem_bytes=60 << 20,
    )
    raw = lax.all_to_all(sent, "yh", 0, 0, tiled=True)
    wown = lax.all_gather(scaled, "z", axis=0, tiled=True)
    raw, wown, lengths, moved, qkv_bias = lax.optimization_barrier((raw, wown, lengths, moved, qkv_bias))

    woth = lax.ppermute(wown, "yl", [(0, 1), (1, 0)])
    raw = lax.optimization_barrier(raw.transpose(1, 0, 2, 3))
    spread = lax.all_to_all(raw, "x", 0, 0, tiled=True)

    squares = jnp.sum(jnp.square(raw.astype(jnp.float32)), axis=(0, 1, 3))
    lens = lengths[0]
    ids = jnp.arange(ROWS, dtype=jnp.int32)
    starts = [jnp.sum(lens[:n]) for n in range(SAMPLES)]
    begin = jnp.zeros_like(ids)
    for n in range(1, SAMPLES):
        begin = jnp.where(ids >= starts[n], starts[n], begin)
    positions = (ids - begin).astype(jnp.float32)
    inv_freq = ROPE_BASE ** (-(2.0 * jnp.arange(HEAD // 2, dtype=jnp.float32)) / HEAD)
    angles = positions[:, None] * inv_freq[None, :]
    cos, sin = jnp.cos(angles), jnp.sin(angles)
    cos = jnp.concatenate([cos, cos], axis=1)
    sin = jnp.concatenate([-sin, sin], axis=1)
    bias = qkv_bias.astype(jnp.float32)[None, :]
    spread, squares, bias, cos, sin = lax.optimization_barrier((spread, squares, bias, cos, sin))
    other = lax.ppermute(spread, "c", [(0, 1), (1, 0)])

    x = lax.axis_index("x")
    whole = lambda step, v: lax.ppermute(v, "x", [(i, (i + step) % NX) for i in range(NX)])
    flops = 2 * ROWS * 1024 * columns
    weights = call(
        arrange_kernel, bf(1024, columns), (c.reshape(1), wown, woth), 1, flops=20 * 10**9, nbytes=3 << 20
    )

    def products(dtype, *steps):
        return call(
            functools.partial(product_kernel, steps),
            (jax.ShapeDtypeStruct((ROWS, columns), dtype),) * len(steps),
            (x.reshape(1), spread, other, weights),
            1,
            flops=len(steps) * flops,
            nbytes=4 << 20,
        )

    (far,) = products(jnp.bfloat16, 2)
    far = whole(2, far)
    right, left = products(jnp.bfloat16, 1, 3)
    (own,) = products(jnp.float32, 0)
    right, left = whole(1, right), whole(3, left)
    own, squares = lax.optimization_barrier((own, squares))
    own = own + far.astype(jnp.float32)
    squares2 = lax.ppermute(squares, "c", [(0, 1), (1, 0)])
    context, sent = call(
        attend_kernel,
        (bf(ROWS, PER * HEAD), bf(ROWS, PER * HEAD)),
        (lens, moved, own, right, left, squares.reshape(1, ROWS), squares2.reshape(1, ROWS), bias, cos, sin),
        2,
        flops=4 * 4 * ROWS * ROWS * HEAD,
        nbytes=3 << 20,
    )
    previous = lax.ppermute(sent, DP, [(i, i + 1) for i in range(NZ * NYL * NX - 1)])
    return call(
        pack_kernel,
        [bf(2 * ROWS, PER * HEAD)],
        (lens, moved, previous, context),
        2,
        flops=4 * 512 * 256 * 512,
        nbytes=1 << 20,
        scratch=[pltpu.VMEM((2, ROWS, PER * HEAD), jnp.bfloat16), pltpu.SemaphoreType.DMA((2,))],
    )[0]


def solution(mesh):
    fine = Mesh(mesh.devices.reshape(NZ, NYL, NX, NYH, NC), DP + TP)
    return jax.shard_map(
        local,
        mesh=fine,
        in_specs=(P(DP, TP), P(DP, None), P(DP), P(), P(DP, TP), P(TP)),
        out_specs=P(DP, TP),
        check_vma=False,
    )
```

```python
import jax
import jax.numpy as jnp
from jax import lax
from jax.experimental import pallas as pl
from jax.experimental.pallas import tpu as pltpu
from jax.sharding import Mesh
from jax.sharding import PartitionSpec as P

HEADS = 32
KV = 8
HEAD = 128
PER = HEADS // KV
EPSILON = 1e-06
ROPE_BASE = 1000000.0

NZ, NYL, NX, NYH, NC = 16, 2, 4, 4, 2
DP = ("z", "yl", "x")
TP = ("yh", "c")
WROWS = 32
ROWS = 256
HALF = 128
SAMPLES = 4
EXTRA = 16
NEAR = (1, 3, 0)
VMEM = 16 << 20


def call(kernel, out_shape, args, scalars=0, hbm=0, flops=0, nbytes=0, scratch=(), vmem_bytes=VMEM):
    smem = pl.BlockSpec(memory_space=pltpu.SMEM)
    vmem = pl.BlockSpec(memory_space=pltpu.VMEM)
    far = pl.BlockSpec(memory_space=pltpu.HBM)
    return pl.pallas_call(
        kernel,
        out_shape=out_shape,
        in_specs=[smem] * scalars + [far] * hbm + [vmem] * (len(args) - scalars - hbm),
        out_specs=[far] * len(out_shape) if isinstance(out_shape, list) else jax.tree.map(lambda _: vmem, out_shape),
        scratch_shapes=list(scratch),
        compiler_params=pltpu.CompilerParams(vmem_limit_bytes=vmem_bytes),
        cost_estimate=pl.CostEstimate(flops=flops, bytes_accessed=nbytes, transcendentals=0),
    )(*args)


def prepare_kernel(yl_ref, dp_ref, s_hbm, w_hbm, gain_ref, o_hbm, ow_hbm, s_ref, w_ref, o_ref, sems):
    halves = [pl.ds(n * HALF, HALF) for n in range(2)]
    loads = [pltpu.make_async_copy(s_hbm.at[rows], s_ref.at[rows], sems.at[n]) for n, rows in enumerate(halves)]
    load_w = pltpu.make_async_copy(w_hbm, w_ref, sems.at[2])
    for copy in (loads[0], load_w, loads[1]):
        copy.start()
    yl, dp = yl_ref[0], dp_ref[0]
    line = lax.broadcasted_iota(jnp.int32, (gain_ref.shape[0], 128), 0)
    gain = jnp.where(line == lax.shift_right_logical(dp, 2), gain_ref[...].astype(jnp.float32), 0.0)
    gain = jnp.sum(gain, axis=0, keepdims=True)
    row = lax.broadcasted_iota(jnp.int32, (WROWS, 128), 0)
    lane = lax.broadcasted_iota(jnp.int32, (WROWS, 128), 1)
    gain = jnp.sum(jnp.where(lane == (dp & 3) * WROWS + row, gain, 0.0), axis=1, keepdims=True)
    source = lax.broadcasted_iota(jnp.int32, (512, 256), 0)
    r = lax.broadcasted_iota(jnp.int32, (512, 256), 1)
    odd, rel, zz, k = [lax.shift_right_logical(r, n) & mask for n, mask in ((7, 1), (6, 1), (5, 1), (0, 31))]
    base = zz * 256 + (rel ^ yl) * 128 + odd * 32 + k
    perms = [(source == base + x * 32).astype(jnp.bfloat16) for x in range(0, NX, 2)]
    stores = []
    for n, rows in enumerate(halves):
        loads[n].wait()
        for x in range(0, NX, 2):
            pair = jnp.dot(s_ref[rows], perms[x // 2], preferred_element_type=jnp.float32).astype(jnp.bfloat16)
            o_ref[x, rows] = pair[:, :128]
            o_ref[x + 1, rows] = pair[:, 128:]
        for yh in range(NYH):
            stores.append(pltpu.make_async_copy(o_ref.at[:, rows], o_hbm.at[yh, :, rows], sems.at[4 + n * NYH + yh]))
            stores[-1].start()
        if n == 0:
            load_w.wait()
            w_ref[...] = (w_ref[...].astype(jnp.float32) * gain).astype(jnp.bfloat16)
            stores.append(pltpu.make_async_copy(w_ref, ow_hbm, sems.at[3]))
            stores[-1].start()
    for copy in stores:
        copy.wait()


def arrange_kernel(c_ref, wown_ref, woth_ref, w_ref):
    c = c_ref[0]
    for rel in range(NC):
        for yh in range(NYH):
            row = pl.multiple_of((yh * 4 + (c ^ rel) * 2) * WROWS, 64)
            at = (rel * NYH + yh) * 128
            w_ref[at : at + 64] = wown_ref[pl.ds(row, 64)]
            w_ref[at + 64 : at + 128] = woth_ref[pl.ds(row, 64)]


def first_kernel(x_at_ref, own_ref, oth_ref, w_ref, o_ref, x_ref):
    x = x_at_ref[0]

    def states(step):
        g = (x + step) & 3
        return jnp.concatenate([ref[g, yh] for ref in (own_ref, oth_ref) for yh in range(NYH)], axis=1)

    o_ref[...] = jnp.dot(states(2), w_ref[...], preferred_element_type=jnp.float32).astype(jnp.bfloat16)
    for n, step in enumerate(NEAR):
        x_ref[n] = states(step)


def second_kernel(x_ref, w_ref, o1_ref, o3_ref):
    for n, ref in enumerate((o1_ref, o3_ref)):
        ref[...] = jnp.dot(x_ref[n], w_ref[...], preferred_element_type=jnp.float32).astype(ref.dtype)


def own_kernel(x_ref, w_ref, o_ref):
    o_ref[...] = jnp.dot(x_ref[2], w_ref[...], preferred_element_type=jnp.float32)


def tail_of(lens, moved):
    return sum(jnp.where(n >= SAMPLES - moved, lens[n], 0) for n in range(SAMPLES))


def attend_kernel(len_ref, moved_ref, p0_ref, p1_ref, p2_ref, sq_ref, sq2_ref, bias_ref, cos_ref, sin_ref, o_ref, sent_ref):
    s1 = len_ref[0]
    s2 = s1 + len_ref[1]
    s3 = s2 + len_ref[2]
    i = lax.broadcasted_iota(jnp.int32, (ROWS, ROWS), 0)
    j = lax.broadcasted_iota(jnp.int32, (ROWS, ROWS), 1)
    start = jnp.where(i >= s3, s3, jnp.where(i >= s2, s2, jnp.where(i >= s1, s1, 0)))
    allowed = (j >= start) & (j <= i)
    r = lax.rsqrt((sq_ref[...] + sq2_ref[...]) * (1.0 / (NZ * NYL * NX * WROWS)) + EPSILON)
    r = jnp.sum(jnp.where(i == j, r, 0.0), axis=1, keepdims=True)
    cos, sin = cos_ref[...], sin_ref[...]

    def head(n):
        at = n * HEAD
        total = p0_ref[:, at : at + HEAD]
        for ref in (p1_ref, p2_ref):
            total = total + ref[:, at : at + HEAD].astype(jnp.float32)
        return total * r + bias_ref[:, n * HEAD : (n + 1) * HEAD]

    def rotate(v, cos, sin):
        return (v * cos + pltpu.roll(v, HEAD // 2, 1) * sin).astype(jnp.bfloat16)

    key = rotate(head(PER), cos, sin)
    cos, sin = cos * HEAD ** (-0.5), sin * HEAD ** (-0.5)
    value = head(PER + 1).astype(jnp.bfloat16)
    for h in range(PER):
        query = rotate(head(h), cos, sin)
        scores = lax.dot_general(query, key, (((1,), (1,)), ((), ())), preferred_element_type=jnp.float32)
        scores = jnp.where(allowed, scores, -1e30)
        e = jnp.exp(scores - jnp.max(scores, axis=1, keepdims=True))
        weights = (e * (1.0 / jnp.sum(e, axis=1, keepdims=True))).astype(jnp.bfloat16)
        o_ref[:, h * HEAD : (h + 1) * HEAD] = jnp.dot(
            weights, value, preferred_element_type=jnp.float32
        ).astype(jnp.bfloat16)
    tail = tail_of(len_ref, moved_ref[0]).astype(jnp.float32)
    sent_ref[EXTRA:] = o_ref[EXTRA:]
    top = o_ref[:EXTRA].astype(jnp.float32)
    row = lax.broadcasted_iota(jnp.int32, top.shape, 0)
    sent_ref[:EXTRA] = jnp.where(row == 0, tail, top).astype(jnp.bfloat16)


def pack_kernel(len_ref, moved_ref, prev_ref, own_ref, o_hbm, o_ref, sems):
    tail = tail_of(len_ref, moved_ref[0])
    incoming = prev_ref[:EXTRA, :HEAD].astype(jnp.float32)[:1, :1].astype(jnp.int32)
    row = lax.broadcasted_iota(jnp.int32, (ROWS, ROWS), 1)
    copies = []
    for block in range(2):
        slot = lax.broadcasted_iota(jnp.int32, (ROWS, ROWS), 0) + block * ROWS
        pick = ((row == slot - incoming) & (row < ROWS - tail)).astype(jnp.bfloat16)
        picked = jnp.dot(pick, own_ref[...], preferred_element_type=jnp.float32)
        if block == 0:
            pick = ((slot < incoming) & (row == slot + (ROWS - incoming))).astype(jnp.bfloat16)
            picked = picked + jnp.dot(pick, prev_ref[...], preferred_element_type=jnp.float32)
        o_ref[block] = picked.astype(jnp.bfloat16)
        copy = pltpu.make_async_copy(o_ref.at[block], o_hbm.at[pl.ds(block * ROWS, ROWS)], sems.at[block])
        copy.start()
        copies.append(copy)
    for copy in copies:
        copy.wait()


def local(states, lengths, moved, norm_gain, qkv_weight, qkv_bias):
    yl, c = lax.axis_index("yl"), lax.axis_index("c")
    dp = lax.axis_index(DP)
    bf = lambda *shape: jax.ShapeDtypeStruct(shape, jnp.bfloat16)

    columns = qkv_weight.shape[1]
    sent, scaled = call(
        prepare_kernel,
        [bf(NYH, NX, ROWS, 128), bf(WROWS, columns)],
        (yl.reshape(1), dp.reshape(1), states, qkv_weight, norm_gain.reshape(-1, 128)),
        2,
        2,
        flops=2 * 256 * 512 * 512,
        nbytes=1 << 20,
        scratch=[
            pltpu.VMEM((ROWS, 512), jnp.bfloat16),
            pltpu.VMEM((WROWS, columns), jnp.bfloat16),
            pltpu.VMEM((NX, ROWS, 128), jnp.bfloat16),
            pltpu.SemaphoreType.DMA((4 + 2 * NYH,)),
        ],
        vmem_bytes=60 << 20,
    )
    raw = lax.all_to_all(sent, "yh", 0, 0, tiled=True)
    wown = lax.all_gather(scaled, "z", axis=0, tiled=True)
    raw, wown, lengths, moved, qkv_bias = lax.optimization_barrier((raw, wown, lengths, moved, qkv_bias))

    woth = lax.ppermute(wown, "yl", [(0, 1), (1, 0)])
    raw = lax.optimization_barrier(raw.transpose(1, 0, 2, 3))
    spread = lax.all_to_all(raw, "x", 0, 0, tiled=True)

    squares = jnp.sum(jnp.square(raw.astype(jnp.float32)), axis=(0, 1, 3))
    lens = lengths[0]
    ids = jnp.arange(ROWS, dtype=jnp.int32)
    starts = [jnp.sum(lens[:n]) for n in range(SAMPLES)]
    begin = jnp.zeros_like(ids)
    for n in range(1, SAMPLES):
        begin = jnp.where(ids >= starts[n], starts[n], begin)
    positions = (ids - begin).astype(jnp.float32)
    inv_freq = ROPE_BASE ** (-(2.0 * jnp.arange(HEAD // 2, dtype=jnp.float32)) / HEAD)
    angles = positions[:, None] * inv_freq[None, :]
    cos, sin = jnp.cos(angles), jnp.sin(angles)
    cos = jnp.concatenate([cos, cos], axis=1)
    sin = jnp.concatenate([-sin, sin], axis=1)
    bias = qkv_bias.astype(jnp.float32)[None, :]
    spread, squares, bias, cos, sin = lax.optimization_barrier((spread, squares, bias, cos, sin))
    other = lax.ppermute(spread, "c", [(0, 1), (1, 0)])

    x = lax.axis_index("x")
    whole = lambda step, v: lax.ppermute(v, "x", [(i, (i + step) % NX) for i in range(NX)])
    flops = 2 * ROWS * 1024 * columns
    weights = call(
        arrange_kernel, bf(1024, columns), (c.reshape(1), wown, woth), 1, flops=20 * 10**9, nbytes=3 << 20
    )
    far, near = call(
        first_kernel,
        (bf(ROWS, columns), bf(3, ROWS, 1024)),
        (x.reshape(1), spread, other, weights),
        1,
        flops=flops,
        nbytes=6 << 20,
    )
    far = whole(2, far)
    right, left = call(
        second_kernel,
        (bf(ROWS, columns), bf(ROWS, columns)),
        (near, weights),
        flops=2 * flops,
        nbytes=4 << 20,
    )
    own = call(
        own_kernel, jax.ShapeDtypeStruct((ROWS, columns), jnp.float32), (near, weights), flops=flops, nbytes=3 << 20
    )
    right, left = whole(1, right), whole(3, left)
    own, squares = lax.optimization_barrier((own, squares))
    own = own + far.astype(jnp.float32)
    squares2 = lax.ppermute(squares, "c", [(0, 1), (1, 0)])
    context, sent = call(
        attend_kernel,
        (bf(ROWS, PER * HEAD), bf(ROWS, PER * HEAD)),
        (lens, moved, own, right, left, squares.reshape(1, ROWS), squares2.reshape(1, ROWS), bias, cos, sin),
        2,
        flops=4 * 4 * ROWS * ROWS * HEAD,
        nbytes=3 << 20,
    )
    previous = lax.ppermute(sent, DP, [(i, i + 1) for i in range(NZ * NYL * NX - 1)])
    return call(
        pack_kernel,
        [bf(2 * ROWS, PER * HEAD)],
        (lens, moved, previous, context),
        2,
        flops=4 * 512 * 256 * 512,
        nbytes=1 << 20,
        scratch=[pltpu.VMEM((2, ROWS, PER * HEAD), jnp.bfloat16), pltpu.SemaphoreType.DMA((2,))],
    )[0]


def solution(mesh):
    fine = Mesh(mesh.devices.reshape(NZ, NYL, NX, NYH, NC), DP + TP)
    return jax.shard_map(
        local,
        mesh=fine,
        in_specs=(P(DP, TP), P(DP, None), P(DP), P(), P(DP, TP), P(TP)),
        out_specs=P(DP, TP),
        check_vma=False,
    )
```
